512 devices in a mesh: chan: 32 (over y, z_hi, core), stn: 16 (over x, z_lo).
Axes of the slice: x: 4, y: 8, z: 8 (z_hi: 2, z_lo: 4; z = z_hi * 4 + z_lo), core: 2. Of those that a mesh axis runs over, the one named last changes fastest.
Arguments:
- voltages: bfloat16 [16, 32, 2, 253952], P('stn', 'chan'), may hold values from -6 to 6
- station_gains: bfloat16 [512, 16, 128], P('chan', 'stn'), may hold values from -3.6 to 3.6
- positions: float32 [512, 2], replicated, may hold values from -64 to 64
- directions: float32 [32, 2], replicated, may hold values from -0.5 to 0.5
- weights: float32 [32, 2], replicated, may hold values from 0.03 to 0.15
- baseline_flags: int32 [512, 512], P('stn'), may hold values from 0 to 1, as said below
Outputs:
- gain_steps: float32 [512, 16, 128], P('chan', 'stn')
The draws below stay inside these ranges and needn't reach their ends.
Inputs may be any that keep to these rules, and one draw needn't show every extreme that they name: symmetric: baseline_flags[s, r] equals baseline_flags[r, s].
All inputs are finite; a program needn't handle non-finite values.
Results may differ from the reference program's by a relative error of at most 0.00099.
Values may be sent and summed in bfloat16 or wider, within the bound.
No kernel may reach another device: no remote copies, remote signals or barrier semaphores. Data moves between devices by JAX's collectives and lax.ppermute only.
A program may use at most 128 MiB of HBM per device.

```python
import math
import jax
import jax.numpy as jnp
from jax import lax

F = 4096
CW = 512
FRAME = 8192
TAPS = 16
STATIONS = 512
POLS = 2
NFRAMES = 16
SOURCES = 32
BLOCKS = 16
SPB = 32
STR_BLK = 64
SAMPLES = 253952


def draw_voltages(key, part):
    key = jax.random.fold_in(key, 11)
    first_key, second_key = jax.random.split(key, 2)
    full_shape = (BLOCKS, SPB, POLS, SAMPLES)
    common = jax.random.normal(first_key, (1, 1, POLS, SAMPLES), jnp.float32)
    own_part = jax.random.normal(second_key, full_shape, jnp.float32)
    mixed = 0.6 * common + 0.8 * own_part
    return jnp.clip(mixed, -6.0, 6.0).astype(jnp.bfloat16)


def draw_station_gains(key, part):
    key = jax.random.fold_in(key, 23)
    first_key, second_key = jax.random.split(key, 2)
    phases = jax.random.uniform(first_key, (CW, BLOCKS, 1, STR_BLK), jnp.float32, -math.pi, math.pi)
    amplitude = jnp.exp(jax.random.uniform(second_key, (CW, BLOCKS, 1, STR_BLK), jnp.float32, math.log(0.3), math.log(3.0)))
    parts_both = jnp.concatenate([amplitude * jnp.cos(phases), amplitude * jnp.sin(phases)], axis=2)
    return parts_both.reshape(CW, BLOCKS, 2 * STR_BLK).astype(jnp.bfloat16)


def draw_baseline_flags(key, part):
    key = jax.random.fold_in(key, 5)
    drawn = jax.random.randint(key, (STATIONS, STATIONS), 0, 3)
    allowed = (drawn > 0).astype(jnp.int32)
    row_ids = jnp.arange(STATIONS, dtype=jnp.int32)[:, None]
    col_ids = jnp.arange(STATIONS, dtype=jnp.int32)[None, :]
    return jnp.where(row_ids < col_ids, allowed, allowed.T)


def setup_inputs(seed: int = 0) -> dict:
    streams_of = jax.random.split(jax.random.key(seed), 7)
    return {
        "voltages": draw_voltages(jax.random.fold_in(streams_of[6], 71), 0),
        "station_gains": draw_station_gains(jax.random.fold_in(streams_of[6], 71), 0),
        "positions": jnp.clip(jax.random.uniform(streams_of[2], (STATIONS, 2), jnp.float32, -64.0, 64.0), -64.0, 64.0),
        "directions": jnp.clip(jax.random.uniform(streams_of[3], (SOURCES, 2), jnp.float32, -0.5, 0.5), -0.5, 0.5),
        "weights": jnp.clip(jnp.exp(jax.random.uniform(streams_of[4], (SOURCES, POLS), jnp.float32, math.log(0.03), math.log(0.15))), 0.03, 0.15),
        "baseline_flags": draw_baseline_flags(jax.random.fold_in(streams_of[6], 71), 0),
    }


def filter_table(tap_count, frame_len):
    total_len = tap_count * frame_len
    sample_ids = jnp.arange(total_len, dtype=jnp.float32)
    offset = (sample_ids + 0.5 - total_len / 2) / frame_len
    window = jnp.sin(jnp.pi * offset) / (jnp.pi * offset) * (0.5 - 0.5 * jnp.cos(2 * jnp.pi * sample_ids / total_len))
    return window.reshape(tap_count, frame_len)

def steering(pos_rows, directions, weights, channels):
    delays = pos_rows[:, 0][:, None] * directions[:, 0][None, :] + pos_rows[:, 1][:, None] * directions[:, 1][None, :]
    scaled = 2.0 * math.pi * (1.0 + channels.astype(jnp.float32) / F)
    phases = scaled[:, None, None] * delays[None]
    real_part = jnp.cos(phases)[..., None] * weights[None, None]
    imag_part = -jnp.sin(phases)[..., None] * weights[None, None]
    stacked = jnp.transpose(jnp.stack([real_part, imag_part], axis=1), (0, 3, 1, 2, 4))
    return stacked.reshape(channels.shape[0], directions.shape[0], -1).astype(jnp.bfloat16)

def block_spectra(block_volts):
    samples = block_volts.reshape(SPB * POLS, NFRAMES + TAPS - 1, FRAME)
    window = filter_table(TAPS, FRAME)
    filtered = jnp.zeros((SPB * POLS, NFRAMES, FRAME), jnp.float32)
    for tap_index in range(TAPS):
        filtered = filtered + samples[:, tap_index:tap_index + NFRAMES, :].astype(jnp.float32) * window[tap_index]
    spectrum = jnp.fft.rfft(filtered, axis=-1)[:, :, :CW] / math.sqrt(FRAME)
    halves = jnp.stack([jnp.real(spectrum), jnp.imag(spectrum)], axis=0)
    return jnp.transpose(halves, (3, 2, 0, 1)).astype(jnp.bfloat16)

def usable_matrix(baseline_flags):
    station_ids = jnp.arange(STATIONS, dtype=jnp.int32)
    allowed = jnp.where(station_ids[:, None] != station_ids[None, :], baseline_flags, 0).astype(jnp.float32)
    allowed = jnp.broadcast_to(allowed[:, None, :, None], (STATIONS, POLS, STATIONS, POLS))
    return allowed.reshape(STATIONS * POLS, STATIONS * POLS)

def reference(voltages, station_gains, positions, directions, weights, baseline_flags):
    spectra = lax.map(block_spectra, voltages)
    streams = STATIONS * POLS
    spectra = jnp.transpose(spectra, (1, 2, 3, 0, 4)).reshape(CW, NFRAMES, 2, streams)
    usable = usable_matrix(baseline_flags)

    def one_channel(inputs):
        chan_spectra, chan_gains, chan_id = inputs
        flat = chan_spectra.astype(jnp.float32).reshape(NFRAMES, 2 * streams)
        product = jnp.dot(flat.T, flat, precision=lax.Precision.HIGHEST, preferred_element_type=jnp.float32)
        vis_re = (product[:streams, :streams] + product[streams:, streams:]) / NFRAMES
        vis_im = (product[streams:, :streams] - product[:streams, streams:]) / NFRAMES
        steer = steering(positions, directions, weights, chan_id[None])[0].astype(jnp.float32)
        model_product = jnp.dot(steer.T, steer, precision=lax.Precision.HIGHEST, preferred_element_type=jnp.float32)
        mod_re = model_product[:streams, :streams] + model_product[streams:, streams:]
        mod_im = model_product[streams:, :streams] - model_product[:streams, streams:]
        gain_re = chan_gains[:, :STR_BLK].astype(jnp.float32).reshape(streams)
        gain_im = chan_gains[:, STR_BLK:].astype(jnp.float32).reshape(streams)
        near_re = gain_re[:, None]
        near_im = gain_im[:, None]
        far_re = gain_re[None, :]
        far_im = gain_im[None, :]
        app_re = far_re * mod_re + far_im * mod_im
        app_im = far_im * mod_re - far_re * mod_im
        pred_re = near_re * app_re + near_im * app_im
        pred_im = near_im * app_re - near_re * app_im
        diff_re = vis_re - pred_re
        diff_im = vis_im - pred_im
        num_re = lax.optimization_barrier(jnp.sum(usable * (diff_re * app_re - diff_im * app_im), axis=1))
        num_im = lax.optimization_barrier(jnp.sum(usable * (diff_re * app_im + diff_im * app_re), axis=1))
        weight_sum = lax.optimization_barrier(jnp.sum(usable * (app_re * app_re + app_im * app_im), axis=1))
        denominator = 1.0 + weight_sum
        return jnp.concatenate([(num_re / denominator).reshape(BLOCKS, STR_BLK), (num_im / denominator).reshape(BLOCKS, STR_BLK)], axis=1)
    return lax.map(one_channel, (spectra, station_gains, jnp.arange(CW, dtype=jnp.int32)))
```

```python
import math

import jax
import jax.numpy as jnp
import numpy as np
from jax import lax
from jax.experimental import pallas as pl
from jax.experimental.pallas import tpu as pltpu
from jax.sharding import PartitionSpec as P

F = 4096
CW = 512
FRAME = 8192
TAPS = 16
STATIONS = 512
NFRAMES = 16
SOURCES = 32
BLOCKS = 16
SPB = 32
FRAMES_IN = NFRAMES + TAPS - 1
BF = jnp.bfloat16
F32 = jnp.float32


def split_np(values):
    hi = values.astype(jnp.bfloat16)
    lo = (values - hi.astype(np.float64)).astype(jnp.bfloat16)
    return hi, lo


def filter_tables():
    n = np.arange(TAPS * FRAME, dtype=np.float64)
    q = (n + 0.5 - TAPS * FRAME / 2) / FRAME
    window = np.sin(np.pi * q) / (np.pi * q) * (0.5 - 0.5 * np.cos(2 * np.pi * n / (TAPS * FRAME)))
    window = window.astype(np.float32).reshape(TAPS, 64, 128)
    k = np.arange(64)[:, None]
    j = np.arange(64)[None, :]
    angle = 2 * np.pi * (k * j % 64) / 64
    first = np.concatenate([np.cos(angle), -np.sin(angle)], axis=0)
    hi, lo = split_np(first)
    first = np.concatenate([hi, hi, lo], axis=1)
    m = np.arange(128)[None, :]
    angle = 2 * np.pi * (k * m % 8192) / 8192
    turn = np.stack([np.cos(angle), np.sin(angle)]).astype(np.float32)
    b = np.arange(8)[None, :]
    mm = np.arange(128)[:, None]
    angle = 2 * np.pi * (b * mm % 128) / 128
    c = np.cos(angle) / math.sqrt(FRAME)
    s = np.sin(angle) / math.sqrt(FRAME)
    to_re = np.concatenate([c, s], axis=0)
    to_im = np.concatenate([-s, c], axis=0)
    second = np.stack([to_re, to_im], axis=2)
    second = np.broadcast_to(second[..., None], (256, 8, 2, NFRAMES)).reshape(256, 256)
    hi, lo = split_np(second)
    return window, first, turn, np.stack([hi, lo])


def split2(x):
    hi = x.astype(BF)
    return hi, (x - hi.astype(F32)).astype(BF)


def dot(a, b):
    return lax.dot_general(a, b, (((1,), (0,)), ((), ())), preferred_element_type=F32)


def dot_nt(a, b):
    return lax.dot_general(a, b, (((1,), (1,)), ((), ())), preferred_element_type=F32)


def iota(shape, dim):
    return lax.broadcasted_iota(jnp.int32, shape, dim)


def spectra_kernel(
    index_ref, volt_ref, win_ref, first_ref, turn_ref, second_ref, gain_ref, flag_ref, out_ref, fold, part
):
    def chunk(step, carry):
        stream = step // 4
        row = pl.multiple_of((step % 4) * 16, 16)
        x = volt_ref[stream, :, pl.ds(row, 16), :].astype(F32)
        acc = x[0:NFRAMES] * win_ref[0, pl.ds(row, 16), :][None]
        for tap in range(1, TAPS):
            acc = acc + x[tap : tap + NFRAMES] * win_ref[tap, pl.ds(row, 16), :][None]
        hi, lo = split2(acc)
        for t in range(NFRAMES):
            fold[stream * NFRAMES + t, pl.ds(row, 16), :] = hi[t]
            fold[stream * NFRAMES + t, pl.ds(pl.multiple_of(row + 64, 16), 16), :] = lo[t]
            fold[stream * NFRAMES + t, pl.ds(pl.multiple_of(row + 128, 16), 16), :] = hi[t]
        return carry

    lax.fori_loop(0, 8, chunk, 0)

    turn_cos = turn_ref[0]
    turn_sin = turn_ref[1]
    first = first_ref[...]
    column = iota((1, 256), 1) % NFRAMES
    total = jnp.zeros((128, 256), F32)
    for t in range(NFRAMES):
        rows = []
        for stream in range(2):
            section = dot(first, fold[stream * NFRAMES + t])
            re, im = section[0:64], section[64:128]
            rows.append(
                jnp.concatenate(
                    [re * turn_cos + im * turn_sin, im * turn_cos - re * turn_sin], axis=1
                )
            )
        hi, lo = split2(jnp.concatenate(rows, axis=0))
        here = jnp.where(column == t, 1.0, 0.0).astype(BF)
        table_hi = second_ref[0] * here
        table_lo = second_ref[1] * here
        total = total + (dot(hi, table_hi) + dot(lo, table_hi) + dot(hi, table_lo))

    index = index_ref[0]
    flags = jnp.broadcast_to(flag_ref[pl.ds(index, 1), :].astype(F32), (8, STATIONS)).astype(BF)
    place = (iota((STATIONS, 384), 1) + 64 * (index // 4)) & (STATIONS - 1)
    wanted = (place & 15) * SPB + lax.shift_right_logical(place, 4)
    pick = jnp.where(iota((STATIONS, 384), 0) == wanted, 1.0, 0.0).astype(BF)
    row = dot(flags, pick)[0:1]

    for b in range(8):
        lanes = [
            total[0:64, b * 32 : b * 32 + 32],
            total[64:128, b * 32 : b * 32 + 32],
            jnp.broadcast_to(row[:, 0:64], (64, 64)),
        ]
        part[pl.ds(b * 256, 64, stride=4), :] = jnp.concatenate(lanes, axis=1)
    part[pl.ds(1, 512, stride=4), :] = jnp.broadcast_to(row[:, 64:192], (512, 128))
    part[pl.ds(2, 512, stride=4), :] = jnp.broadcast_to(row[:, 192:320], (512, 128))
    gains = gain_ref[...].astype(F32)
    for i in range(32):
        part[pl.ds(i * 64 + 3, 16, stride=4), :] = gains
    out_ref[...] = part[...].astype(BF)


def pair_kernel(
    index_ref, recv_ref, cos_ref, sin_ref, weight_ref, out_ref, part, near_x, near_e, far_e, usable, acc
):
    part[...] = recv_ref[...].astype(F32)
    first = part[pl.ds(0, 512, stride=4), :]
    index = index_ref[0]

    sent = jnp.concatenate(
        [
            first[:, 64:128],
            part[pl.ds(1, 512, stride=4), :],
            part[pl.ds(2, 512, stride=4), :],
        ],
        axis=1,
    )
    empty = jnp.zeros((64, 64), F32)
    for a in range(8):
        pieces = []
        for b in range(8):
            d = (b - a) % 8
            pieces.append(sent[a * 64 : a * 64 + 64, d * 64 : d * 64 + 64] if d <= 4 else empty)
        usable[pl.ds(a * 64, 64), :] = jnp.concatenate(pieces, axis=1)
    brought = usable[...]
    rows, cols = iota((512, 512), 0), iota((512, 512), 1)
    ahead = (lax.shift_right_logical(cols, 6) - lax.shift_right_logical(rows, 6)) & 7
    both = jnp.where(ahead <= 4, brought, brought.T)
    usable[...] = jnp.where(rows == cols, 0.0, both)

    xt = first.T
    zero32 = jnp.zeros((32, 512), F32)
    for p in range(2):
        own = xt[p * 32 : p * 32 + 32]
        other = jnp.concatenate([own[16:32], -own[0:16]], axis=0)
        for c, block in enumerate((own, other)):
            for q in range(2):
                whole = [zero32, zero32, zero32, zero32]
                whole[q] = block
                near_x[p, c, q] = jnp.concatenate(whole, axis=0).astype(BF)

    cos, sin = cos_ref[...], sin_ref[...]
    zero64 = jnp.zeros((64, 512), F32)
    steer, turned = [], []
    for p in range(2):
        weight = weight_ref[:, p : p + 1]
        re = (cos * weight).astype(BF).astype(F32)
        im = (-sin * weight).astype(BF).astype(F32)
        steer += [re, im]
        turned += [-im, re]
        for c, block in enumerate(((re, im), (-im, re))):
            for q in range(2):
                half = [zero64, zero64]
                half[q] = jnp.concatenate(block, axis=0)
                near_e[p, c, q] = jnp.concatenate(half + half, axis=0).astype(BF)
    steer = jnp.concatenate(steer, axis=0).T
    turned = jnp.concatenate(turned, axis=0).T

    gains = part[pl.ds(index * 64 + 3, 16, stride=4), :].astype(BF)
    to_row = jnp.where((iota((512, 16), 0) & 15) == iota((512, 16), 1), 1.0, 0.0).astype(BF)
    spread = dot(to_row, gains)
    lane = iota((512, 128), 1)
    own_lane = lax.shift_right_logical(lane & 63, 1) == lax.shift_right_logical(iota((512, 128), 0), 4)
    spread = jnp.where(own_lane, spread, 0.0).astype(BF)
    source = iota((128, 256), 0)
    target = iota((128, 256), 1)
    fits = ((source & 1) == (lax.shift_right_logical(target, 6) & 1)) & (
        lax.shift_right_logical(source, 6) == lax.shift_right_logical(target, 7)
    )
    wide = dot(spread, jnp.where(fits, 1.0, 0.0).astype(BF))
    scaled = wide[:, 0:128] * steer + wide[:, 128:256] * turned
    hi, lo = split2(scaled)
    far_e[:, 0:128] = hi
    far_e[:, 128:256] = lo
    far_x = first.astype(BF)
    code = iota((8, 128), 0)
    lane = iota((8, 128), 1)
    fits = ((lane & 1) == (code & 1)) & (lax.shift_right_logical(lane, 6) == lax.shift_right_logical(code, 1))
    near_gain = dot_nt(jnp.where(fits, 1.0, 0.0).astype(BF), spread)

    for p in range(2):
        for half in range(2):
            cols = slice(half * 256, half * 256 + 256)
            sums = [jnp.zeros((8, 256), F32)] * 3
            for q in range(2):
                for r in range(4):
                    rows = slice(r * 128, r * 128 + 128)
                    vr = dot(far_x[rows], near_x[p, 0, q, :, cols])
                    vi = dot(far_x[rows], near_x[p, 1, q, :, cols])
                    ar = dot(far_e[rows, :], near_e[p, 0, q, :, cols])
                    ai = dot(far_e[rows, :], near_e[p, 1, q, :, cols])
                    mask = usable[rows, cols]
                    ur, ui = mask * ar, mask * ai
                    terms = (vr * ur - vi * ui, vr * ui + vi * ur, ur * ur + ui * ui)
                    sums = [s + jnp.sum(t.reshape(16, 8, 256), axis=0) for s, t in zip(sums, terms)]
            for n in range(3):
                acc[n, p, :, cols] = sums[n]

    steps = []
    for part_id in range(2):
        for p in range(2):
            weight_sum = jnp.sum(acc[2, p], axis=0, keepdims=True)
            moment = jnp.sum(acc[part_id, p], axis=0, keepdims=True) * (1.0 / NFRAMES)
            own = near_gain[part_id * 2 + p : part_id * 2 + p + 1]
            steps.append((moment - own * weight_sum) / (1.0 + weight_sum))

    mine = (iota((16, 512), 1) & 15) == iota((16, 512), 0)
    source = iota((512, 128), 0)
    target = iota((512, 128), 1)
    placed = jnp.zeros((48, 128), F32)
    for n, value in enumerate(steps):
        value = jnp.where(mine, jnp.broadcast_to(value, (16, 512)), 0.0)
        hi = value.astype(BF)
        rest = value - hi.astype(F32)
        mid = rest.astype(BF)
        low = (rest - mid.astype(F32)).astype(BF)
        column = (n // 2) * 64 + lax.shift_right_logical(source, 4) * 2 + (n % 2)
        move = jnp.where(target == column, 1.0, 0.0).astype(BF)
        placed = placed + dot(jnp.concatenate([hi, mid, low], axis=0), move)
    out_ref[...] = placed[0:16] + (placed[16:32] + placed[32:48])


def whole():
    return pl.BlockSpec(memory_space=pltpu.VMEM)


def make_spectra(index, volts, gains, flags):
    window, first, turn, second = filter_tables()
    return pl.pallas_call(
        spectra_kernel,
        out_shape=jax.ShapeDtypeStruct((4 * CW, 128), BF),
        in_specs=[pl.BlockSpec(memory_space=pltpu.SMEM)] + [whole()] * 7,
        out_specs=whole(),
        scratch_shapes=[pltpu.VMEM((32, 192, 128), BF), pltpu.VMEM((4 * CW, 128), F32)],
        compiler_params=pltpu.CompilerParams(vmem_limit_bytes=48 * 2**20),
        name="spectra",
    )(index, volts, jnp.asarray(window), jnp.asarray(first), jnp.asarray(turn), jnp.asarray(second), gains, flags)


def make_steps(index, recv, cos, sin, weights):
    return pl.pallas_call(
        pair_kernel,
        out_shape=jax.ShapeDtypeStruct((BLOCKS, 128), F32),
        in_specs=[pl.BlockSpec(memory_space=pltpu.SMEM)] + [whole()] * 4,
        out_specs=whole(),
        scratch_shapes=[
            pltpu.VMEM((4 * STATIONS, 128), F32),
            pltpu.VMEM((2, 2, 2, 128, STATIONS), BF),
            pltpu.VMEM((2, 2, 2, 256, STATIONS), BF),
            pltpu.VMEM((STATIONS, 256), BF),
            pltpu.VMEM((STATIONS, STATIONS), F32),
            pltpu.VMEM((3, 2, 8, STATIONS), F32),
        ],
        compiler_params=pltpu.CompilerParams(vmem_limit_bytes=48 * 2**20),
        name="pairs",
    )(index, recv, cos, sin, weights)


def steering_phases(positions, directions, channel):
    order = positions.reshape(BLOCKS, SPB, 2).transpose(2, 1, 0).reshape(2, STATIONS)
    delays = order[0][None, :] * directions[:, 0][:, None] + order[1][None, :] * directions[:, 1][:, None]
    scaled = 2.0 * math.pi * (1.0 + channel.astype(F32) / F)
    phases = scaled * delays
    return jnp.cos(phases), jnp.sin(phases)


def body(voltages, station_gains, positions, directions, weights, baseline_flags):
    chan_index = lax.axis_index("chan")
    stn_index = lax.axis_index("stn")
    index = jnp.reshape(chan_index, (1,)).astype(jnp.int32)
    channel = chan_index * BLOCKS + stn_index
    volts = voltages.reshape(2, FRAMES_IN, 64, 128)
    payload = make_spectra(index, volts, station_gains[:, 0, :], baseline_flags)
    recv = lax.all_to_all(
        payload.reshape(CW, 4, 128), ("chan", "stn"), split_axis=0, concat_axis=0, tiled=True
    )
    cos, sin = steering_phases(positions, directions, channel)
    steps = make_steps(index, recv.reshape(4 * CW, 128), cos, sin, weights)
    return lax.all_to_all(steps.reshape(BLOCKS, 1, 128), "stn", split_axis=0, concat_axis=0, tiled=True)


def solution(mesh):
    in_specs = (P("stn", "chan", None, None), P("chan", "stn", None), P(), P(), P(), P("stn", None))
    out_specs = P("chan", "stn", None)
    return jax.shard_map(body, mesh=mesh, in_specs=in_specs, out_specs=out_specs, check_vma=False)
```

```python
import math

import jax
import jax.numpy as jnp
import numpy as np
from jax import lax
from jax.experimental import pallas as pl
from jax.experimental.pallas import tpu as pltpu
from jax.sharding import PartitionSpec as P

F = 4096
CW = 512
FRAME = 8192
TAPS = 16
STATIONS = 512
NFRAMES = 16
SOURCES = 32
BLOCKS = 16
SPB = 32
FRAMES_IN = NFRAMES + TAPS - 1
CHUNKS = 8
CHUNK = 16
ROWS = 256
BF = jnp.bfloat16
F32 = jnp.float32


def split_np(values):
    hi = values.astype(jnp.bfloat16)
    lo = (values - hi.astype(np.float64)).astype(jnp.bfloat16)
    return hi, lo


def filter_tables():
    n = np.arange(TAPS * FRAME, dtype=np.float64)
    q = (n + 0.5 - TAPS * FRAME / 2) / FRAME
    window = np.sin(np.pi * q) / (np.pi * q) * (0.5 - 0.5 * np.cos(2 * np.pi * n / (TAPS * FRAME)))
    window = window.astype(np.float32).reshape(TAPS, 64, 128)
    window = np.repeat(window, 2, axis=1).reshape(TAPS, CHUNKS, 16, 128).transpose(1, 0, 2, 3)
    j = np.arange(64)[:, None]
    k = np.arange(64)[None, :]
    angle = 2 * np.pi * (k * j % 64) / 64
    first = np.stack([np.cos(angle), -np.sin(angle)])
    first = np.einsum("cjk,st->jsctk", first, np.eye(2)).reshape(128, 256)
    hi, lo = split_np(first)
    first = np.concatenate([hi, hi, lo], axis=0)
    m = np.arange(128)[:, None]
    angle = 2 * np.pi * (k * m % 8192) / 8192
    turn = np.stack([np.cos(angle), np.sin(angle)])
    turn = np.concatenate([turn, turn], axis=2).astype(np.float32)
    b = np.arange(8)[:, None]
    m = np.arange(128)[None, :]
    angle = 2 * np.pi * (b * m % 128) / 128
    c = np.cos(angle) / math.sqrt(FRAME)
    s = np.sin(angle) / math.sqrt(FRAME)
    to_re = np.concatenate([c, s], axis=1)
    to_im = np.concatenate([-s, c], axis=1)
    second = np.stack([to_re, to_im], axis=1).reshape(16, 256)
    second = np.concatenate(split_np(second), axis=0)
    return window, first, turn, second


def split2(x):
    hi = x.astype(BF)
    return hi, (x - hi.astype(F32)).astype(BF)


def dot(a, b):
    return lax.dot_general(a, b, (((1,), (0,)), ((), ())), preferred_element_type=F32)


def dot_nt(a, b):
    return lax.dot_general(a, b, (((1,), (1,)), ((), ())), preferred_element_type=F32)


def iota(shape, dim):
    return lax.broadcasted_iota(jnp.int32, shape, dim)


def spectra_kernel(
    index_ref,
    volt_ref,
    win_ref,
    first_ref,
    turn_ref,
    second_ref,
    gain_ref,
    flag_ref,
    out_ref,
    volts,
    window,
    first,
    turn,
    second,
    gain,
    flag,
    fold,
    gathered,
    part,
    ready,
    sems,
    late,
    left,
    section,
    high,
    low,
):

    def volt_copy(step):
        rows = pl.ds(pl.multiple_of(step * 16, 16), 16)
        return pltpu.make_async_copy(volt_ref.at[:, rows, :], volts.at[step], sems.at[0, step])

    def window_copy(step):
        return pltpu.make_async_copy(win_ref.at[step], window.at[step], sems.at[1, step])

    early = [
        pltpu.make_async_copy(source, target, late.at[n])
        for n, (source, target) in enumerate(((gain_ref, gain), (flag_ref, flag)))
    ]
    others = [
        pltpu.make_async_copy(source, target, late.at[n + 2])
        for n, (source, target) in enumerate(((first_ref, first), (turn_ref, turn), (second_ref, second)))
    ]
    volt_copy(0).start()
    window_copy(0).start()
    for copy in early:
        copy.start()
    for step in range(1, CHUNKS):
        volt_copy(step).start()
        window_copy(step).start()
    for copy in others:
        copy.start()

    index = index_ref[0]
    place = (iota((1, 384), 1) + 64 * (index // 4)) & (STATIONS - 1)
    wanted = (place & 15) * SPB + lax.shift_right_logical(place, 4)
    pick = jnp.where(iota((STATIONS, 384), 0) == wanted, 1.0, 0.0).astype(BF)
    for copy in early:
        copy.wait()
    flags = jnp.broadcast_to(flag[pl.ds(index, 1), :].astype(F32), (8, STATIONS)).astype(BF)
    row = dot(flags, pick)[0:1]
    part[pl.ds(1, 512, stride=4), :] = jnp.broadcast_to(row[:, 64:192], (512, 128))
    part[pl.ds(2, 512, stride=4), :] = jnp.broadcast_to(row[:, 192:320], (512, 128))
    gains = gain[...].astype(F32)
    for i in range(32):
        part[pl.ds(i * 64 + 3, 16, stride=4), :] = gains

    def chunk(step, carry):
        volt_copy(step).wait()
        window_copy(step).wait()
        x = volts[step].astype(F32)
        acc = x[0:NFRAMES] * window[step, 0][None]
        for tap in range(1, TAPS):
            acc = acc + x[tap : tap + NFRAMES] * window[step, tap][None]
        fold[:, pl.ds(pl.multiple_of(step * 16, 16), 16), :] = acc
        return carry

    lax.fori_loop(0, CHUNKS, chunk, 0)
    for copy in others:
        copy.wait()

    turn_cos = turn[0]
    turn_sin = turn[1]
    for t in range(NFRAMES):
        hi, lo = split2(fold[t].T)
        rows = slice(t * 128, t * 128 + 128)
        left[rows, 0:128] = hi
        left[rows, 128:256] = lo
    for group in range(4):
        rows = slice(group * 512, group * 512 + 512)
        section[rows, :] = dot(left[rows, :], first[0:256]) + dot(left[rows, 0:128], first[256:384])
    for t in range(NFRAMES):
        rows = slice(t * 128, t * 128 + 128)
        re = section[rows, 0:128]
        im = section[rows, 128:256]
        for part_id, value in enumerate((re * turn_cos + im * turn_sin, im * turn_cos - re * turn_sin)):
            hi, lo = split2(value)
            place = slice(part_id * 128, part_id * 128 + 128)
            high[place, rows] = hi
            low[place, rows] = lo
    main = dot(second[...], high[...])
    rest = dot(second[0:16], low[...])
    value = main[0:16] + (main[16:32] + rest)
    for t in range(NFRAMES):
        gathered[pl.ds(t, 16, stride=16), :] = value[:, t * 128 : t * 128 + 128]
    total = gathered[...].T

    copies = []
    for b in range(8):
        lanes = [
            total[0:64, b * 32 : b * 32 + 32],
            total[64:128, b * 32 : b * 32 + 32],
            jnp.broadcast_to(row[:, 0:64], (64, 64)),
        ]
        rows = pl.ds(b * 256, 256)
        part[pl.ds(b * 256, 64, stride=4), :] = jnp.concatenate(lanes, axis=1)
        ready[rows, :] = part[rows, :].astype(BF)
        copies.append(pltpu.make_async_copy(ready.at[rows, :], out_ref.at[rows, :], sems.at[0, b]))
        copies[-1].start()
    for copy in copies:
        copy.wait()


def steer_kernel(cos_ref, sin_ref, weight_ref, near_e, steer_ref, turned_ref):
    cos, sin = cos_ref[...], sin_ref[...]
    steer, turned = [], []
    for p in range(2):
        weight = weight_ref[:, p : p + 1]
        re = (cos * weight).astype(BF).astype(F32)
        im = (-sin * weight).astype(BF).astype(F32)
        steer += [re, im]
        turned += [-im, re]
        near_e[p, 0] = jnp.concatenate([re, im, re, im], axis=0).astype(BF)
        near_e[p, 1] = jnp.concatenate([-im, re, -im, re], axis=0).astype(BF)
    steer_ref[...] = jnp.concatenate(steer, axis=0).T
    turned_ref[...] = jnp.concatenate(turned, axis=0).T


def pair_kernel(
    index_ref, recv_ref, near_e, steer_ref, turned_ref, out_ref, part, near_x, far_x, far_e, usable, acc, *products
):
    part[...] = recv_ref[...].astype(F32)
    first = part[pl.ds(0, 512, stride=4), :]
    index = index_ref[0]

    sent = jnp.concatenate(
        [
            first[:, 64:128],
            part[pl.ds(1, 512, stride=4), :],
            part[pl.ds(2, 512, stride=4), :],
        ],
        axis=1,
    )
    empty = jnp.zeros((64, 64), F32)
    for a in range(8):
        pieces = []
        for b in range(8):
            d = (b - a) % 8
            pieces.append(sent[a * 64 : a * 64 + 64, d * 64 : d * 64 + 64] if d <= 4 else empty)
        usable[pl.ds(a * 64, 64), :] = jnp.concatenate(pieces, axis=1)
    brought = usable[...]
    rows, cols = iota((512, 512), 0), iota((512, 512), 1)
    ahead = (lax.shift_right_logical(cols, 6) - lax.shift_right_logical(rows, 6)) & 7
    both = jnp.where(ahead <= 4, brought, brought.T)
    usable[...] = jnp.where(rows == cols, 0.0, both)

    xt = first.T
    for p in range(2):
        own = xt[p * 32 : p * 32 + 32]
        near_x[p, 0] = own.astype(BF)
        near_x[p, 1] = jnp.concatenate([own[16:32], -own[0:16]], axis=0).astype(BF)
        far_x[p] = first[:, p * 32 : p * 32 + 32].astype(BF)

    gains = part[pl.ds(index * 64 + 3, 16, stride=4), :].astype(BF)
    to_row = jnp.where((iota((512, 16), 0) & 15) == iota((512, 16), 1), 1.0, 0.0).astype(BF)
    spread = dot(to_row, gains)
    lane = iota((512, 128), 1)
    own_lane = lax.shift_right_logical(lane & 63, 1) == lax.shift_right_logical(iota((512, 128), 0), 4)
    spread = jnp.where(own_lane, spread, 0.0).astype(BF)
    source = iota((128, 256), 0)
    target = iota((128, 256), 1)
    fits = ((source & 1) == (lax.shift_right_logical(target, 6) & 1)) & (
        lax.shift_right_logical(source, 6) == lax.shift_right_logical(target, 7)
    )
    wide = dot(spread, jnp.where(fits, 1.0, 0.0).astype(BF))
    scaled = wide[:, 0:128] * steer_ref[...] + wide[:, 128:256] * turned_ref[...]
    for q in range(2):
        hi, lo = split2(scaled[:, q * 64 : q * 64 + 64])
        far_e[q] = jnp.concatenate([hi, lo], axis=1)
    code = iota((8, 128), 0)
    lane = iota((8, 128), 1)
    fits = ((lane & 1) == (code & 1)) & (lax.shift_right_logical(lane, 6) == lax.shift_right_logical(code, 1))
    near_gain = dot_nt(jnp.where(fits, 1.0, 0.0).astype(BF), spread)

    blocks = [(p, half, q) for p in range(2) for half in range(2) for q in range(2)]
    sums = {}
    for n in range(len(blocks) + 1):
        for r in range(0, STATIONS, ROWS):
            rows = slice(r, r + ROWS)
            if n < len(blocks):
                p, half, q = blocks[n]
                cols = slice(half * 256, half * 256 + 256)
                vr, vi, ar, ai = products[4 * (n % 2) : 4 * (n % 2) + 4]
                vr[rows, :] = dot(far_x[q, rows], near_x[p, 0, :, cols])
                vi[rows, :] = dot(far_x[q, rows], near_x[p, 1, :, cols])
                ar[rows, :] = dot(far_e[q, rows], near_e[p, 0, :, cols])
                ai[rows, :] = dot(far_e[q, rows], near_e[p, 1, :, cols])
            if n > 0:
                p, half, q = blocks[n - 1]
                cols = slice(half * 256, half * 256 + 256)
                vr, vi, ar, ai = products[4 * ((n - 1) % 2) : 4 * ((n - 1) % 2) + 4]
                total = sums.get((p, half), [jnp.zeros((8, 256), F32)] * 3)
                for c in range(r, r + ROWS, CHUNK):
                    some = slice(c, c + CHUNK)
                    mask = usable[some, cols]
                    ur, ui = mask * ar[some, :], mask * ai[some, :]
                    xr, xi = vr[some, :], vi[some, :]
                    terms = (xr * ur - xi * ui, xr * ui + xi * ur, ur * ur + ui * ui)
                    total = [s + jnp.sum(t.reshape(CHUNK // 8, 8, 256), axis=0) for s, t in zip(total, terms)]
                sums[p, half] = total
    for (p, half), total in sums.items():
        for n in range(3):
            acc[n, p, :, half * 256 : half * 256 + 256] = total[n]

    steps = []
    for part_id in range(2):
        for p in range(2):
            weight_sum = jnp.sum(acc[2, p], axis=0, keepdims=True)
            moment = jnp.sum(acc[part_id, p], axis=0, keepdims=True) * (1.0 / NFRAMES)
            own = near_gain[part_id * 2 + p : part_id * 2 + p + 1]
            steps.append((moment - own * weight_sum) / (1.0 + weight_sum))

    mine = (iota((16, 512), 1) & 15) == iota((16, 512), 0)
    source = iota((512, 128), 0)
    target = iota((512, 128), 1)
    placed = jnp.zeros((48, 128), F32)
    for n, value in enumerate(steps):
        value = jnp.where(mine, jnp.broadcast_to(value, (16, 512)), 0.0)
        hi = value.astype(BF)
        rest = value - hi.astype(F32)
        mid = rest.astype(BF)
        low = (rest - mid.astype(F32)).astype(BF)
        column = (n // 2) * 64 + lax.shift_right_logical(source, 4) * 2 + (n % 2)
        move = jnp.where(target == column, 1.0, 0.0).astype(BF)
        placed = placed + dot(jnp.concatenate([hi, mid, low], axis=0), move)
    out_ref[...] = placed[0:16] + (placed[16:32] + placed[32:48])


def whole():
    return pl.BlockSpec(memory_space=pltpu.VMEM)


def anywhere():
    return pl.BlockSpec(memory_space=pltpu.HBM)


def make_spectra(index, volts, gains, flags):
    window, first, turn, second = filter_tables()
    return pl.pallas_call(
        spectra_kernel,
        out_shape=jax.ShapeDtypeStruct((4 * CW, 128), BF),
        in_specs=[pl.BlockSpec(memory_space=pltpu.SMEM)] + [anywhere()] * 7,
        out_specs=anywhere(),
        scratch_shapes=[
            pltpu.VMEM((CHUNKS, FRAMES_IN, 16, 128), BF),
            pltpu.VMEM((CHUNKS, TAPS, 16, 128), F32),
            pltpu.VMEM((384, 256), BF),
            pltpu.VMEM((2, 128, 128), F32),
            pltpu.VMEM((32, 256), BF),
            pltpu.VMEM((BLOCKS, 128), BF),
            pltpu.VMEM((SPB, STATIONS), jnp.int32),
            pltpu.VMEM((NFRAMES, 128, 128), F32),
            pltpu.VMEM((256, 128), F32),
            pltpu.VMEM((4 * CW, 128), F32),
            pltpu.VMEM((4 * CW, 128), BF),
            pltpu.SemaphoreType.DMA((2, CHUNKS)),
            pltpu.SemaphoreType.DMA((5,)),
            pltpu.VMEM((NFRAMES * 128, 256), BF),
            pltpu.VMEM((NFRAMES * 128, 256), F32),
            pltpu.VMEM((256, NFRAMES * 128), BF),
            pltpu.VMEM((256, NFRAMES * 128), BF),
        ],
        compiler_params=pltpu.CompilerParams(vmem_limit_bytes=60 * 2**20),
        name="spectra",
    )(index, volts, jnp.asarray(window), jnp.asarray(first), jnp.asarray(turn), jnp.asarray(second), gains, flags)


def arrange(voltages):
    rows = voltages.reshape(2, FRAMES_IN * 64, 128).transpose(1, 0, 2)
    return rows.reshape(FRAMES_IN, 128, 128)


def make_steering(cos, sin, weights):
    return pl.pallas_call(
        steer_kernel,
        out_shape=(
            jax.ShapeDtypeStruct((2, 2, 128, STATIONS), BF),
            jax.ShapeDtypeStruct((STATIONS, 128), F32),
            jax.ShapeDtypeStruct((STATIONS, 128), F32),
        ),
        in_specs=[whole()] * 3,
        out_specs=(whole(),) * 3,
        compiler_params=pltpu.CompilerParams(vmem_limit_bytes=16 * 2**20),
        name="steer",
    )(cos, sin, weights)


def make_steps(index, recv, near_e, steer, turned):
    return pl.pallas_call(
        pair_kernel,
        out_shape=jax.ShapeDtypeStruct((BLOCKS, 128), F32),
        in_specs=[pl.BlockSpec(memory_space=pltpu.SMEM)] + [whole()] * 4,
        out_specs=whole(),
        scratch_shapes=[
            pltpu.VMEM((4 * STATIONS, 128), F32),
            pltpu.VMEM((2, 2, 32, STATIONS), BF),
            pltpu.VMEM((2, STATIONS, 32), BF),
            pltpu.VMEM((2, STATIONS, 128), BF),
            pltpu.VMEM((STATIONS, STATIONS), F32),
            pltpu.VMEM((3, 2, 8, STATIONS), F32),
        ]
        + [pltpu.VMEM((STATIONS, 256), F32)] * 8,
        compiler_params=pltpu.CompilerParams(vmem_limit_bytes=24 * 2**20),
        name="pairs",
    )(index, recv, near_e, steer, turned)


def steering_phases(positions, directions, channel):
    order = positions.reshape(BLOCKS, SPB, 2).transpose(2, 1, 0).reshape(2, STATIONS)
    delays = order[0][None, :] * directions[:, 0][:, None] + order[1][None, :] * directions[:, 1][:, None]
    scaled = 2.0 * math.pi * (1.0 + channel.astype(F32) / F)
    phases = scaled * delays
    return jnp.cos(phases), jnp.sin(phases)


def body(voltages, station_gains, positions, directions, weights, baseline_flags):
    chan_index = lax.axis_index("chan")
    stn_index = lax.axis_index("stn")
    index = jnp.reshape(chan_index, (1,)).astype(jnp.int32)
    channel = chan_index * BLOCKS + stn_index
    volts = arrange(voltages)
    payload = make_spectra(index, volts, station_gains[:, 0, :], baseline_flags)
    recv = lax.all_to_all(
        payload.reshape(CW, 4, 128), ("chan", "stn"), split_axis=0, concat_axis=0, tiled=True
    )
    cos, sin = steering_phases(positions, directions, channel)
    steps = make_steps(index, recv.reshape(4 * CW, 128), *make_steering(cos, sin, weights))
    return lax.all_to_all(steps.reshape(BLOCKS, 1, 128), "stn", split_axis=0, concat_axis=0, tiled=True)


def solution(mesh):
    in_specs = (P("stn", "chan", None, None), P("chan", "stn", None), P(), P(), P(), P("stn", None))
    out_specs = P("chan", "stn", None)
    return jax.shard_map(body, mesh=mesh, in_specs=in_specs, out_specs=out_specs, check_vma=False)
```

```python
import math

import jax
import jax.numpy as jnp
import numpy as np
from jax import lax
from jax.experimental import pallas as pl
from jax.experimental.pallas import tpu as pltpu
from jax.sharding import Mesh
from jax.sharding import PartitionSpec as P

F = 4096
CW = 512
FRAME = 8192
TAPS = 16
STATIONS = 512
NFRAMES = 16
SOURCES = 32
BLOCKS = 16
SPB = 32
FRAMES_IN = NFRAMES + TAPS - 1
CHUNKS = 8
CHUNK = 16
ROWS = 256
CHAN = ("y", "z_hi", "core")
STN = ("x", "z_lo")
BF = jnp.bfloat16
F32 = jnp.float32


def split_np(values):
    hi = values.astype(jnp.bfloat16)
    lo = (values - hi.astype(np.float64)).astype(jnp.bfloat16)
    return hi, lo


def filter_tables():
    n = np.arange(TAPS * FRAME, dtype=np.float64)
    q = (n + 0.5 - TAPS * FRAME / 2) / FRAME
    window = np.sin(np.pi * q) / (np.pi * q) * (0.5 - 0.5 * np.cos(2 * np.pi * n / (TAPS * FRAME)))
    window = window.astype(np.float32).reshape(TAPS, 64, 128)
    window = np.repeat(window, 2, axis=1).reshape(TAPS, CHUNKS, 16, 128).transpose(1, 0, 2, 3)
    j = np.arange(64)[:, None]
    k = np.arange(64)[None, :]
    angle = 2 * np.pi * (k * j % 64) / 64
    first = np.stack([np.cos(angle), -np.sin(angle)])
    first = np.einsum("cjk,st->jsctk", first, np.eye(2)).reshape(128, 256)
    hi, lo = split_np(first)
    first = np.concatenate([hi, hi, lo], axis=0)
    m = np.arange(128)[:, None]
    angle = 2 * np.pi * (k * m % 8192) / 8192
    turn = np.stack([np.cos(angle), np.sin(angle)])
    turn = np.concatenate([turn, turn], axis=2).astype(np.float32)
    b = np.arange(8)[:, None]
    m = np.arange(128)[None, :]
    angle = 2 * np.pi * (b * m % 128) / 128
    c = np.cos(angle) / math.sqrt(FRAME)
    s = np.sin(angle) / math.sqrt(FRAME)
    to_re = np.concatenate([c, s], axis=1)
    to_im = np.concatenate([-s, c], axis=1)
    second = np.stack([to_re, to_im], axis=1).reshape(16, 256)
    second = np.concatenate(split_np(second), axis=0)
    return window, first, turn, second


def split2(x):
    hi = x.astype(BF)
    return hi, (x - hi.astype(F32)).astype(BF)


def dot(a, b):
    return lax.dot_general(a, b, (((1,), (0,)), ((), ())), preferred_element_type=F32)


def dot_nt(a, b):
    return lax.dot_general(a, b, (((1,), (1,)), ((), ())), preferred_element_type=F32)


def iota(shape, dim):
    return lax.broadcasted_iota(jnp.int32, shape, dim)


def spectra_kernel(
    volt_ref,
    win_ref,
    first_ref,
    turn_ref,
    second_ref,
    out_ref,
    volts,
    window,
    first,
    turn,
    second,
    fold,
    left,
    section,
    high,
    low,
    gathered,
    sems,
    late,
):
    def volt_copy(step):
        rows = pl.ds(pl.multiple_of(step * 16, 16), 16)
        return pltpu.make_async_copy(volt_ref.at[:, rows, :], volts.at[step], sems.at[0, step])

    def window_copy(step):
        return pltpu.make_async_copy(win_ref.at[step], window.at[step], sems.at[1, step])

    others = [
        pltpu.make_async_copy(source, target, late.at[n])
        for n, (source, target) in enumerate(
            ((first_ref, first), (turn_ref, turn), (second_ref, second))
        )
    ]
    for step in range(CHUNKS):
        volt_copy(step).start()
        window_copy(step).start()
    for copy in others:
        copy.start()

    def chunk(step, carry):
        volt_copy(step).wait()
        window_copy(step).wait()
        x = volts[step].astype(F32)
        acc = x[0:NFRAMES] * window[step, 0][None]
        for tap in range(1, TAPS):
            acc = acc + x[tap : tap + NFRAMES] * window[step, tap][None]
        fold[:, pl.ds(pl.multiple_of(step * 16, 16), 16), :] = acc
        return carry

    lax.fori_loop(0, CHUNKS, chunk, 0)
    for copy in others:
        copy.wait()

    turn_cos = turn[0]
    turn_sin = turn[1]
    for t in range(NFRAMES):
        hi, lo = split2(fold[t].T)
        rows = slice(t * 128, t * 128 + 128)
        left[rows, 0:128] = hi
        left[rows, 128:256] = lo
    for group in range(4):
        rows = slice(group * 512, group * 512 + 512)
        section[rows, :] = dot(left[rows, :], first[0:256]) + dot(left[rows, 0:128], first[256:384])
    for t in range(NFRAMES):
        rows = slice(t * 128, t * 128 + 128)
        re = section[rows, 0:128]
        im = section[rows, 128:256]
        for part_id, value in enumerate((re * turn_cos + im * turn_sin, im * turn_cos - re * turn_sin)):
            hi, lo = split2(value)
            place = slice(part_id * 128, part_id * 128 + 128)
            high[place, rows] = hi
            low[place, rows] = lo
    main = dot(second[...], high[...])
    rest = dot(second[0:16], low[...])
    value = main[0:16] + (main[16:32] + rest)
    for t in range(NFRAMES):
        gathered[pl.ds(t, 16, stride=16), :] = value[:, t * 128 : t * 128 + 128]
    total = gathered[...].T

    rest = jnp.zeros((64, 64), F32)
    for b in range(8):
        lanes = [total[0:64, b * 32 : b * 32 + 32], total[64:128, b * 32 : b * 32 + 32], rest]
        rows = jnp.concatenate(lanes, axis=1).astype(BF)
        for n, k in enumerate((0, 2, 1, 3)):
            out_ref[b * 64 + n * 16 : b * 64 + n * 16 + 16, :] = rows[k * 16 : k * 16 + 16]


def station_part(n):
    return (lax.shift_right_logical(n, 1) & 7) * 4 + lax.shift_right_logical(n, 8) * 2 + (n & 1)


def station_block(n):
    return lax.shift_right_logical(n, 4) & 15


def flag_kernel(index_ref, flag_ref, out_ref):
    half, block = index_ref[0], index_ref[1]
    source = iota((16, SPB), 0)
    wanted = lax.shift_right_logical(source, 1) * 4 + half * 2 + (source & 1)
    rows = jnp.where(iota((16, SPB), 1) == wanted, 1.0, 0.0).astype(BF)
    flags = dot(rows, flag_ref[...].astype(F32).astype(BF)).astype(BF)
    place = (iota((1, 384), 1) + 256 * half + 64 * (block // 4)) & (STATIONS - 1)
    wanted = station_block(place) * SPB + station_part(place)
    pick = jnp.where(iota((STATIONS, 384), 0) == wanted, 1.0, 0.0).astype(BF)
    out_ref[...] = dot(flags, pick)


def forward_kernel(recv_ref, flag_ref, gain_ref, out_ref, part):
    low = iota((32, 128), 1) < 64
    gains = gain_ref[...].astype(F32)
    for n in range(16):
        flags = flag_ref[n : n + 1, :]
        spectra = recv_ref[n * 32 : n * 32 + 32, :].astype(F32)
        start = jnp.concatenate([flags[:, 0:64], flags[:, 0:64]], axis=1)
        part[pl.ds(n * 4, 32, stride=64), :] = jnp.where(low, spectra, jnp.broadcast_to(start, (32, 128)))
        part[pl.ds(n * 4 + 1, 32, stride=64), :] = jnp.broadcast_to(flags[:, 64:192], (32, 128))
        part[pl.ds(n * 4 + 2, 32, stride=64), :] = jnp.broadcast_to(flags[:, 192:320], (32, 128))
        part[pl.ds(n * 4 + 3, 16, stride=64), :] = gains
        part[pl.ds(n * 4 + 1027, 16, stride=64), :] = gains
    out_ref[...] = part[...].astype(BF)


def steer_kernel(cos_ref, sin_ref, weight_ref, near_e, steer_ref, turned_ref):
    cos, sin = cos_ref[...], sin_ref[...]
    steer, turned = [], []
    for p in range(2):
        weight = weight_ref[:, p : p + 1]
        re = (cos * weight).astype(BF).astype(F32)
        im = (-sin * weight).astype(BF).astype(F32)
        steer += [re, im]
        turned += [-im, re]
        near_e[p, 0] = jnp.concatenate([re, im, re, im], axis=0).astype(BF)
        near_e[p, 1] = jnp.concatenate([-im, re, -im, re], axis=0).astype(BF)
    steer_ref[...] = jnp.concatenate(steer, axis=0).T
    turned_ref[...] = jnp.concatenate(turned, axis=0).T


def pair_kernel(
    index_ref, recv_ref, near_e, steer_ref, turned_ref, out_ref, part, near_x, far_x, far_e, usable, acc, *products
):
    part[...] = recv_ref[...].astype(F32)
    first = part[pl.ds(0, 512, stride=4), :]
    half = index_ref[0]

    sent = jnp.concatenate(
        [
            first[:, 64:128],
            part[pl.ds(1, 512, stride=4), :],
            part[pl.ds(2, 512, stride=4), :],
        ],
        axis=1,
    )
    empty = jnp.zeros((64, 64), F32)
    for a in range(8):
        pieces = []
        for b in range(8):
            d = (b - a) % 8
            pieces.append(sent[a * 64 : a * 64 + 64, d * 64 : d * 64 + 64] if d <= 4 else empty)
        usable[pl.ds(a * 64, 64), :] = jnp.concatenate(pieces, axis=1)
    brought = usable[...]
    rows, cols = iota((512, 512), 0), iota((512, 512), 1)
    ahead = (lax.shift_right_logical(cols, 6) - lax.shift_right_logical(rows, 6)) & 7
    both = jnp.where(ahead <= 4, brought, brought.T)
    usable[...] = jnp.where(rows == cols, 0.0, both)

    xt = first.T
    for p in range(2):
        own = xt[p * 32 : p * 32 + 32]
        near_x[p, 0] = own.astype(BF)
        near_x[p, 1] = jnp.concatenate([own[16:32], -own[0:16]], axis=0).astype(BF)
        far_x[p] = first[:, p * 32 : p * 32 + 32].astype(BF)

    gains = part[pl.ds(half * 1024 + 3, 16, stride=64), :].astype(BF)
    to_row = jnp.where(station_block(iota((512, 16), 0)) == iota((512, 16), 1), 1.0, 0.0).astype(BF)
    spread = dot(to_row, gains)
    lane = iota((512, 128), 1)
    own_lane = lax.shift_right_logical(lane & 63, 1) == station_part(iota((512, 128), 0))
    spread = jnp.where(own_lane, spread, 0.0).astype(BF)
    source = iota((128, 256), 0)
    target = iota((128, 256), 1)
    fits = ((source & 1) == (lax.shift_right_logical(target, 6) & 1)) & (
        lax.shift_right_logical(source, 6) == lax.shift_right_logical(target, 7)
    )
    wide = dot(spread, jnp.where(fits, 1.0, 0.0).astype(BF))
    scaled = wide[:, 0:128] * steer_ref[...] + wide[:, 128:256] * turned_ref[...]
    for q in range(2):
        hi, lo = split2(scaled[:, q * 64 : q * 64 + 64])
        far_e[q] = jnp.concatenate([hi, lo], axis=1)
    code = iota((8, 128), 0)
    lane = iota((8, 128), 1)
    fits = ((lane & 1) == (code & 1)) & (lax.shift_right_logical(lane, 6) == lax.shift_right_logical(code, 1))
    near_gain = dot_nt(jnp.where(fits, 1.0, 0.0).astype(BF), spread)

    blocks = [(p, half, q) for p in range(2) for half in range(2) for q in range(2)]
    sums = {}
    for n in range(len(blocks) + 1):
        for r in range(0, STATIONS, ROWS):
            rows = slice(r, r + ROWS)
            if n < len(blocks):
                p, half, q = blocks[n]
                cols = slice(half * 256, half * 256 + 256)
                vr, vi, ar, ai = products[4 * (n % 2) : 4 * (n % 2) + 4]
                vr[rows, :] = dot(far_x[q, rows], near_x[p, 0, :, cols])
                vi[rows, :] = dot(far_x[q, rows], near_x[p, 1, :, cols])
                ar[rows, :] = dot(far_e[q, rows], near_e[p, 0, :, cols])
                ai[rows, :] = dot(far_e[q, rows], near_e[p, 1, :, cols])
            if n > 0:
                p, half, q = blocks[n - 1]
                cols = slice(half * 256, half * 256 + 256)
                vr, vi, ar, ai = products[4 * ((n - 1) % 2) : 4 * ((n - 1) % 2) + 4]
                total = sums.get((p, half), [jnp.zeros((8, 256), F32)] * 3)
                for c in range(r, r + ROWS, CHUNK):
                    some = slice(c, c + CHUNK)
                    mask = usable[some, cols]
                    ur, ui = mask * ar[some, :], mask * ai[some, :]
                    xr, xi = vr[some, :], vi[some, :]
                    terms = (xr * ur - xi * ui, xr * ui + xi * ur, ur * ur + ui * ui)
                    total = [s + jnp.sum(t.reshape(CHUNK // 8, 8, 256), axis=0) for s, t in zip(total, terms)]
                sums[p, half] = total
    for (p, half), total in sums.items():
        for n in range(3):
            acc[n, p, :, half * 256 : half * 256 + 256] = total[n]

    steps = []
    for part_id in range(2):
        for p in range(2):
            weight_sum = jnp.sum(acc[2, p], axis=0, keepdims=True)
            moment = jnp.sum(acc[part_id, p], axis=0, keepdims=True) * (1.0 / NFRAMES)
            own = near_gain[part_id * 2 + p : part_id * 2 + p + 1]
            steps.append((moment - own * weight_sum) / (1.0 + weight_sum))

    mine = station_block(iota((16, 512), 1)) == iota((16, 512), 0)
    source = station_part(iota((512, 128), 0)) * 2
    target = iota((512, 128), 1)
    placed = jnp.zeros((48, 128), F32)
    for n, value in enumerate(steps):
        value = jnp.where(mine, jnp.broadcast_to(value, (16, 512)), 0.0)
        hi = value.astype(BF)
        rest = value - hi.astype(F32)
        mid = rest.astype(BF)
        low = (rest - mid.astype(F32)).astype(BF)
        column = (n // 2) * 64 + source + (n % 2)
        move = jnp.where(target == column, 1.0, 0.0).astype(BF)
        placed = placed + dot(jnp.concatenate([hi, mid, low], axis=0), move)
    out_ref[...] = placed[0:16] + (placed[16:32] + placed[32:48])


def whole():
    return pl.BlockSpec(memory_space=pltpu.VMEM)


def anywhere():
    return pl.BlockSpec(memory_space=pltpu.HBM)


def make_spectra(volts):
    window, first, turn, second = filter_tables()
    return pl.pallas_call(
        spectra_kernel,
        out_shape=jax.ShapeDtypeStruct((CW, 128), BF),
        in_specs=[anywhere()] * 5,
        out_specs=whole(),
        scratch_shapes=[
            pltpu.VMEM((CHUNKS, FRAMES_IN, 16, 128), BF),
            pltpu.VMEM((CHUNKS, TAPS, 16, 128), F32),
            pltpu.VMEM((384, 256), BF),
            pltpu.VMEM((2, 128, 128), F32),
            pltpu.VMEM((32, 256), BF),
            pltpu.VMEM((NFRAMES, 128, 128), F32),
            pltpu.VMEM((NFRAMES * 128, 256), BF),
            pltpu.VMEM((NFRAMES * 128, 256), F32),
            pltpu.VMEM((256, NFRAMES * 128), BF),
            pltpu.VMEM((256, NFRAMES * 128), BF),
            pltpu.VMEM((256, 128), F32),
            pltpu.SemaphoreType.DMA((2, CHUNKS)),
            pltpu.SemaphoreType.DMA((3,)),
        ],
        compiler_params=pltpu.CompilerParams(vmem_limit_bytes=60 * 2**20),
        name="spectra",
    )(volts, jnp.asarray(window), jnp.asarray(first), jnp.asarray(turn), jnp.asarray(second))


def make_flags(index, flags):
    return pl.pallas_call(
        flag_kernel,
        out_shape=jax.ShapeDtypeStruct((16, 384), F32),
        in_specs=[pl.BlockSpec(memory_space=pltpu.SMEM), whole()],
        out_specs=whole(),
        compiler_params=pltpu.CompilerParams(vmem_limit_bytes=16 * 2**20),
        name="flags",
    )(index, flags)


def make_forward(recv, flags, gains):
    return pl.pallas_call(
        forward_kernel,
        out_shape=jax.ShapeDtypeStruct((4 * STATIONS, 128), BF),
        in_specs=[whole()] * 3,
        out_specs=whole(),
        scratch_shapes=[pltpu.VMEM((4 * STATIONS, 128), F32)],
        compiler_params=pltpu.CompilerParams(vmem_limit_bytes=16 * 2**20),
        name="forward",
    )(recv, flags, gains)


def arrange(voltages):
    rows = voltages.reshape(2, FRAMES_IN * 64, 128).transpose(1, 0, 2)
    return rows.reshape(FRAMES_IN, 128, 128)


def make_steering(cos, sin, weights):
    return pl.pallas_call(
        steer_kernel,
        out_shape=(
            jax.ShapeDtypeStruct((2, 2, 128, STATIONS), BF),
            jax.ShapeDtypeStruct((STATIONS, 128), F32),
            jax.ShapeDtypeStruct((STATIONS, 128), F32),
        ),
        in_specs=[whole()] * 3,
        out_specs=(whole(),) * 3,
        compiler_params=pltpu.CompilerParams(vmem_limit_bytes=16 * 2**20),
        name="steer",
    )(cos, sin, weights)


def make_steps(index, recv, near_e, steer, turned):
    return pl.pallas_call(
        pair_kernel,
        out_shape=jax.ShapeDtypeStruct((BLOCKS, 128), F32),
        in_specs=[pl.BlockSpec(memory_space=pltpu.SMEM)] + [whole()] * 4,
        out_specs=whole(),
        scratch_shapes=[
            pltpu.VMEM((4 * STATIONS, 128), F32),
            pltpu.VMEM((2, 2, 32, STATIONS), BF),
            pltpu.VMEM((2, STATIONS, 32), BF),
            pltpu.VMEM((2, STATIONS, 128), BF),
            pltpu.VMEM((STATIONS, STATIONS), F32),
            pltpu.VMEM((3, 2, 8, STATIONS), F32),
        ]
        + [pltpu.VMEM((STATIONS, 256), F32)] * 8,
        compiler_params=pltpu.CompilerParams(vmem_limit_bytes=24 * 2**20),
        name="pairs",
    )(index, recv, near_e, steer, turned)


def steering_phases(positions, directions, channel):
    order = positions.reshape(BLOCKS, 8, 2, 2, 2).transpose(4, 2, 0, 1, 3).reshape(2, STATIONS)
    delays = order[0][None, :] * directions[:, 0][:, None] + order[1][None, :] * directions[:, 1][:, None]
    scaled = 2.0 * math.pi * (1.0 + channel.astype(F32) / F)
    phases = scaled * delays
    return jnp.cos(phases), jnp.sin(phases)


def exchange(values, axes):
    return lax.all_to_all(values, axes, split_axis=0, concat_axis=0, tiled=True)


def body(voltages, station_gains, positions, directions, weights, baseline_flags):
    half = lax.axis_index("z_hi")
    stn_index = lax.axis_index(STN)
    index = jnp.stack([half, stn_index]).astype(jnp.int32)
    channel = lax.axis_index(CHAN) * BLOCKS + stn_index
    spectra = make_spectra(arrange(voltages)).reshape(16, 32, 128)
    halfway = exchange(spectra, ("y", "core")).reshape(CW, 128)
    flags = make_flags(index, baseline_flags)
    payload = make_forward(halfway, flags, station_gains[:, 0, :])
    recv = exchange(payload.reshape(32, 64, 128), ("z_hi",) + STN).reshape(4 * STATIONS, 128)
    cos, sin = steering_phases(positions, directions, channel)
    steps = make_steps(index, recv, *make_steering(cos, sin, weights))
    return exchange(steps.reshape(BLOCKS, 1, 128), STN)


def solution(mesh):
    parts = Mesh(mesh.devices.reshape(8, 2, 2, 4, 4), CHAN + STN)
    in_specs = (P(STN, CHAN, None, None), P(CHAN, STN, None), P(), P(), P(), P(STN, None))
    out_specs = P(CHAN, STN, None)
    return jax.shard_map(body, mesh=parts, in_specs=in_specs, out_specs=out_specs, check_vma=False)
```

```python
import math

import jax
import jax.numpy as jnp
import numpy as np
from jax import lax
from jax.experimental import pallas as pl
from jax.experimental.pallas import tpu as pltpu
from jax.sharding import PartitionSpec as P

F = 4096
CW = 512
FRAME = 8192
TAPS = 16
STATIONS = 512
NFRAMES = 16
SOURCES = 32
BLOCKS = 16
SPB = 32
FRAMES_IN = NFRAMES + TAPS - 1
CHUNKS = 8
CHUNK = 16
ROWS = 256
BF = jnp.bfloat16
F32 = jnp.float32


def split_np(values):
    hi = values.astype(jnp.bfloat16)
    lo = (values - hi.astype(np.float64)).astype(jnp.bfloat16)
    return hi, lo


def filter_tables():
    n = np.arange(TAPS * FRAME, dtype=np.float64)
    q = (n + 0.5 - TAPS * FRAME / 2) / FRAME
    window = np.sin(np.pi * q) / (np.pi * q) * (0.5 - 0.5 * np.cos(2 * np.pi * n / (TAPS * FRAME)))
    window = window.astype(np.float32).reshape(TAPS, 64, 128)
    window = np.repeat(window, 2, axis=1).reshape(TAPS, CHUNKS, 16, 128).transpose(1, 0, 2, 3)
    j = np.arange(64)[:, None]
    k = np.arange(64)[None, :]
    angle = 2 * np.pi * (k * j % 64) / 64
    first = np.stack([np.cos(angle), -np.sin(angle)])
    first = np.einsum("cjk,st->jsctk", first, np.eye(2)).reshape(128, 256)
    hi, lo = split_np(first)
    first = np.concatenate([hi, hi, lo], axis=0)
    m = np.arange(128)[:, None]
    angle = 2 * np.pi * (k * m % 8192) / 8192
    turn = np.stack([np.cos(angle), np.sin(angle)])
    turn = np.concatenate([turn, turn], axis=2).astype(np.float32)
    b = np.arange(8)[:, None]
    m = np.arange(128)[None, :]
    angle = 2 * np.pi * (b * m % 128) / 128
    c = np.cos(angle) / math.sqrt(FRAME)
    s = np.sin(angle) / math.sqrt(FRAME)
    to_re = np.concatenate([c, s], axis=1)
    to_im = np.concatenate([-s, c], axis=1)
    second = np.stack([to_re, to_im], axis=1).reshape(16, 256)
    second = np.concatenate(split_np(second), axis=0)
    return window, first, turn, second


def split2(x):
    hi = x.astype(BF)
    return hi, (x - hi.astype(F32)).astype(BF)


def dot(a, b):
    return lax.dot_general(a, b, (((1,), (0,)), ((), ())), preferred_element_type=F32)


def dot_nt(a, b):
    return lax.dot_general(a, b, (((1,), (1,)), ((), ())), preferred_element_type=F32)


def iota(shape, dim):
    return lax.broadcasted_iota(jnp.int32, shape, dim)


def spectra_kernel(
    index_ref,
    volt_ref,
    win_ref,
    first_ref,
    turn_ref,
    second_ref,
    gain_ref,
    flag_ref,
    out_ref,
    volts,
    window,
    first,
    turn,
    second,
    gain,
    flag,
    pick,
    fold,
    left,
    section,
    high,
    low,
    gathered,
    part,
    sems,
    late,
):
    def volt_copy(step):
        rows = pl.ds(pl.multiple_of(step * 16, 16), 16)
        return pltpu.make_async_copy(volt_ref.at[:, rows, :], volts.at[step], sems.at[0, step])

    def window_copy(step):
        return pltpu.make_async_copy(win_ref.at[step], window.at[step], sems.at[1, step])

    others = [
        pltpu.make_async_copy(source, target, late.at[n])
        for n, (source, target) in enumerate(
            ((first_ref, first), (turn_ref, turn), (second_ref, second), (gain_ref, gain), (flag_ref, flag))
        )
    ]
    for step in range(CHUNKS):
        volt_copy(step).start()
        window_copy(step).start()
    for copy in others:
        copy.start()

    index = index_ref[0]
    place = (iota((1, 384), 1) + 64 * (index // 4)) & (STATIONS - 1)
    wanted = (place & 15) * SPB + lax.shift_right_logical(place, 4)
    pick[...] = jnp.where(iota((STATIONS, 384), 0) == wanted, 1.0, 0.0).astype(BF)

    def chunk(step, carry):
        volt_copy(step).wait()
        window_copy(step).wait()
        x = volts[step].astype(F32)
        acc = x[0:NFRAMES] * window[step, 0][None]
        for tap in range(1, TAPS):
            acc = acc + x[tap : tap + NFRAMES] * window[step, tap][None]
        fold[:, pl.ds(pl.multiple_of(step * 16, 16), 16), :] = acc
        return carry

    lax.fori_loop(0, CHUNKS, chunk, 0)
    for copy in others:
        copy.wait()

    turn_cos = turn[0]
    turn_sin = turn[1]
    for t in range(NFRAMES):
        hi, lo = split2(fold[t].T)
        rows = slice(t * 128, t * 128 + 128)
        left[rows, 0:128] = hi
        left[rows, 128:256] = lo
    for group in range(4):
        rows = slice(group * 512, group * 512 + 512)
        section[rows, :] = dot(left[rows, :], first[0:256]) + dot(left[rows, 0:128], first[256:384])
    for t in range(NFRAMES):
        rows = slice(t * 128, t * 128 + 128)
        re = section[rows, 0:128]
        im = section[rows, 128:256]
        for part_id, value in enumerate((re * turn_cos + im * turn_sin, im * turn_cos - re * turn_sin)):
            hi, lo = split2(value)
            place = slice(part_id * 128, part_id * 128 + 128)
            high[place, rows] = hi
            low[place, rows] = lo
    main = dot(second[...], high[...])
    rest = dot(second[0:16], low[...])
    value = main[0:16] + (main[16:32] + rest)
    for t in range(NFRAMES):
        gathered[pl.ds(t, 16, stride=16), :] = value[:, t * 128 : t * 128 + 128]
    total = gathered[...].T

    flags = jnp.broadcast_to(flag[pl.ds(index, 1), :].astype(F32), (8, STATIONS)).astype(BF)
    row = dot(flags, pick[...])[0:1]

    for b in range(8):
        lanes = [
            total[0:64, b * 32 : b * 32 + 32],
            total[64:128, b * 32 : b * 32 + 32],
            jnp.broadcast_to(row[:, 0:64], (64, 64)),
        ]
        part[pl.ds(b * 256, 64, stride=4), :] = jnp.concatenate(lanes, axis=1)
    part[pl.ds(1, 512, stride=4), :] = jnp.broadcast_to(row[:, 64:192], (512, 128))
    part[pl.ds(2, 512, stride=4), :] = jnp.broadcast_to(row[:, 192:320], (512, 128))
    gains = gain[...].astype(F32)
    for i in range(32):
        part[pl.ds(i * 64 + 3, 16, stride=4), :] = gains
    out_ref[...] = part[...].astype(BF)


def steer_kernel(
    cos_ref, sin_ref, weight_ref, near_e, steer_ref, turned_ref, own_ref, row_ref, wide_ref, code_ref, move_ref
):
    cos, sin = cos_ref[...], sin_ref[...]
    steer, turned = [], []
    for p in range(2):
        weight = weight_ref[:, p : p + 1]
        re = (cos * weight).astype(BF).astype(F32)
        im = (-sin * weight).astype(BF).astype(F32)
        steer += [re, im]
        turned += [-im, re]
        near_e[p, 0] = jnp.concatenate([re, im, re, im], axis=0).astype(BF)
        near_e[p, 1] = jnp.concatenate([-im, re, -im, re], axis=0).astype(BF)
    steer_ref[...] = jnp.concatenate(steer, axis=0).T
    turned_ref[...] = jnp.concatenate(turned, axis=0).T
    station = iota((STATIONS, 128), 0)
    lane = iota((STATIONS, 128), 1)
    place, block = lax.shift_right_logical(station, 4), station & 15
    own_ref[...] = jnp.where(lax.shift_right_logical(lane & 63, 1) == place, 1.0, 0.0)
    row_ref[...] = jnp.where(block == lane, 1.0, 0.0).astype(BF)
    source = iota((128, 256), 0)
    target = iota((128, 256), 1)
    fits = ((source & 1) == (lax.shift_right_logical(target, 6) & 1)) & (
        lax.shift_right_logical(source, 6) == lax.shift_right_logical(target, 7)
    )
    wide_ref[...] = jnp.where(fits, 1.0, 0.0).astype(BF)
    code = iota((16, 128), 0)
    lane = iota((16, 128), 1)
    fits = ((lane & 1) == (code & 1)) & (lax.shift_right_logical(lane, 6) == lax.shift_right_logical(code, 1))
    code_ref[...] = jnp.where(fits, 1.0, 0.0).astype(BF)
    for n in range(4):
        column = (n // 2) * 64 + place * 2 + (n % 2)
        move_ref[n] = jnp.where(iota((STATIONS, 128), 1) == column, 1.0, 0.0).astype(BF)


def pair_kernel(
    index_ref,
    recv_ref,
    near_e,
    steer_ref,
    turned_ref,
    own_ref,
    row_ref,
    wide_ref,
    code_ref,
    move_ref,
    out_ref,
    part,
    near_x,
    far_x,
    far_e,
    brought,
    usable,
    acc,
    *products,
):
    part[...] = recv_ref[...].astype(F32)
    first = part[pl.ds(0, 512, stride=4), :]
    index = index_ref[0]

    sent = jnp.concatenate(
        [
            first[:, 64:128],
            part[pl.ds(1, 512, stride=4), :],
            part[pl.ds(2, 512, stride=4), :],
        ],
        axis=1,
    )
    empty = jnp.zeros((64, 64), F32)
    for a in range(8):
        pieces = []
        for b in range(8):
            d = (b - a) % 8
            pieces.append(sent[a * 64 : a * 64 + 64, d * 64 : d * 64 + 64] if d <= 4 else empty)
        brought[pl.ds(a * 64, 64), :] = jnp.concatenate(pieces, axis=1)
    turned = brought[...].T
    low = iota((64, 128), 1) < 64
    for a in range(8):
        rows = slice(a * 64, a * 64 + 64)
        for b in range(0, 8, 2):
            cols = slice(b * 64, b * 64 + 128)
            direct, back = brought[rows, cols], turned[rows, cols]
            known = [(n - a) % 8 <= 4 for n in (b, b + 1)]
            if known == [True, True]:
                both = direct
            elif known == [False, False]:
                both = back
            else:
                both = jnp.where(low == known[0], direct, back)
            if a // 2 == b // 2:
                both = jnp.where(iota((64, 128), 0) + (a - b) * 64 == iota((64, 128), 1), 0.0, both)
            usable[rows, cols] = both

    xt = first.T
    for p in range(2):
        own = xt[p * 32 : p * 32 + 32]
        near_x[p, 0] = own.astype(BF)
        near_x[p, 1] = jnp.concatenate([own[16:32], -own[0:16]], axis=0).astype(BF)
        far_x[p] = first[:, p * 32 : p * 32 + 32].astype(BF)

    gains = part[pl.ds(index * 64 + 3, 16, stride=4), :].astype(BF)
    gains = jnp.concatenate([gains, jnp.zeros((112, 128), BF)], axis=0)
    spread = (dot(row_ref[...], gains) * own_ref[...]).astype(BF)
    wide = dot(spread, wide_ref[...])
    scaled = wide[:, 0:128] * steer_ref[...] + wide[:, 128:256] * turned_ref[...]
    for q in range(2):
        hi, lo = split2(scaled[:, q * 64 : q * 64 + 64])
        far_e[q] = jnp.concatenate([hi, lo], axis=1)
    near_gain = dot_nt(code_ref[...], spread)

    blocks = [(p, half, q) for p in range(2) for half in range(2) for q in range(2)]
    sums = {}
    for n in range(len(blocks) + 1):
        for r in range(0, STATIONS, ROWS):
            rows = slice(r, r + ROWS)
            if n < len(blocks):
                p, half, q = blocks[n]
                cols = slice(half * 256, half * 256 + 256)
                vr, vi, ar, ai = products[4 * (n % 2) : 4 * (n % 2) + 4]
                vr[rows, :] = dot(far_x[q, rows], near_x[p, 0, :, cols])
                vi[rows, :] = dot(far_x[q, rows], near_x[p, 1, :, cols])
                ar[rows, :] = dot(far_e[q, rows], near_e[p, 0, :, cols])
                ai[rows, :] = dot(far_e[q, rows], near_e[p, 1, :, cols])
            if n > 0:
                p, half, q = blocks[n - 1]
                cols = slice(half * 256, half * 256 + 256)
                vr, vi, ar, ai = products[4 * ((n - 1) % 2) : 4 * ((n - 1) % 2) + 4]
                total = sums.get((p, half), [jnp.zeros((8, 256), F32)] * 3)
                for c in range(r, r + ROWS, CHUNK):
                    some = slice(c, c + CHUNK)
                    mask = usable[some, cols]
                    ur, ui = mask * ar[some, :], mask * ai[some, :]
                    xr, xi = vr[some, :], vi[some, :]
                    terms = (xr * ur - xi * ui, xr * ui + xi * ur, ur * ur + ui * ui)
                    total = [s + jnp.sum(t.reshape(CHUNK // 8, 8, 256), axis=0) for s, t in zip(total, terms)]
                sums[p, half] = total
    for (p, half), total in sums.items():
        for n in range(3):
            acc[n, p, :, half * 256 : half * 256 + 256] = total[n]

    steps = []
    for part_id in range(2):
        for p in range(2):
            weight_sum = jnp.sum(acc[2, p], axis=0, keepdims=True)
            moment = jnp.sum(acc[part_id, p], axis=0, keepdims=True) * (1.0 / NFRAMES)
            own = near_gain[part_id * 2 + p : part_id * 2 + p + 1]
            steps.append((moment - own * weight_sum) / (1.0 + weight_sum))

    mine = (iota((16, 512), 1) & 15) == iota((16, 512), 0)
    placed = jnp.zeros((48, 128), F32)
    for n, value in enumerate(steps):
        value = jnp.where(mine, jnp.broadcast_to(value, (16, 512)), 0.0)
        hi = value.astype(BF)
        rest = value - hi.astype(F32)
        mid = rest.astype(BF)
        low = (rest - mid.astype(F32)).astype(BF)
        placed = placed + dot(jnp.concatenate([hi, mid, low], axis=0), move_ref[n])
    out_ref[...] = placed[0:16] + (placed[16:32] + placed[32:48])


def whole():
    return pl.BlockSpec(memory_space=pltpu.VMEM)


def anywhere():
    return pl.BlockSpec(memory_space=pltpu.HBM)


def make_spectra(index, volts, gains, flags):
    window, first, turn, second = filter_tables()
    return pl.pallas_call(
        spectra_kernel,
        out_shape=jax.ShapeDtypeStruct((4 * CW, 128), BF),
        in_specs=[pl.BlockSpec(memory_space=pltpu.SMEM)] + [anywhere()] * 7,
        out_specs=whole(),
        scratch_shapes=[
            pltpu.VMEM((CHUNKS, FRAMES_IN, 16, 128), BF),
            pltpu.VMEM((CHUNKS, TAPS, 16, 128), F32),
            pltpu.VMEM((384, 256), BF),
            pltpu.VMEM((2, 128, 128), F32),
            pltpu.VMEM((32, 256), BF),
            pltpu.VMEM((BLOCKS, 128), BF),
            pltpu.VMEM((SPB, STATIONS), jnp.int32),
            pltpu.VMEM((STATIONS, 384), BF),
            pltpu.VMEM((NFRAMES, 128, 128), F32),
            pltpu.VMEM((NFRAMES * 128, 256), BF),
            pltpu.VMEM((NFRAMES * 128, 256), F32),
            pltpu.VMEM((256, NFRAMES * 128), BF),
            pltpu.VMEM((256, NFRAMES * 128), BF),
            pltpu.VMEM((256, 128), F32),
            pltpu.VMEM((4 * CW, 128), F32),
            pltpu.SemaphoreType.DMA((2, CHUNKS)),
            pltpu.SemaphoreType.DMA((5,)),
        ],
        compiler_params=pltpu.CompilerParams(vmem_limit_bytes=60 * 2**20),
        name="spectra",
    )(index, volts, jnp.asarray(window), jnp.asarray(first), jnp.asarray(turn), jnp.asarray(second), gains, flags)


def arrange(voltages):
    rows = voltages.reshape(2, FRAMES_IN * 64, 128).transpose(1, 0, 2)
    return rows.reshape(FRAMES_IN, 128, 128)


def make_steering(cos, sin, weights):
    return pl.pallas_call(
        steer_kernel,
        out_shape=(
            jax.ShapeDtypeStruct((2, 2, 128, STATIONS), BF),
            jax.ShapeDtypeStruct((STATIONS, 128), F32),
            jax.ShapeDtypeStruct((STATIONS, 128), F32),
            jax.ShapeDtypeStruct((STATIONS, 128), F32),
            jax.ShapeDtypeStruct((STATIONS, 128), BF),
            jax.ShapeDtypeStruct((128, 256), BF),
            jax.ShapeDtypeStruct((16, 128), BF),
            jax.ShapeDtypeStruct((4, STATIONS, 128), BF),
        ),
        in_specs=[whole()] * 3,
        out_specs=(whole(),) * 8,
        compiler_params=pltpu.CompilerParams(vmem_limit_bytes=16 * 2**20),
        name="steer",
    )(cos, sin, weights)


def make_steps(index, recv, *prepared):
    return pl.pallas_call(
        pair_kernel,
        out_shape=jax.ShapeDtypeStruct((BLOCKS, 128), F32),
        in_specs=[pl.BlockSpec(memory_space=pltpu.SMEM)] + [whole()] * 9,
        out_specs=whole(),
        scratch_shapes=[
            pltpu.VMEM((4 * STATIONS, 128), F32),
            pltpu.VMEM((2, 2, 32, STATIONS), BF),
            pltpu.VMEM((2, STATIONS, 32), BF),
            pltpu.VMEM((2, STATIONS, 128), BF),
            pltpu.VMEM((STATIONS, STATIONS), F32),
            pltpu.VMEM((STATIONS, STATIONS), F32),
            pltpu.VMEM((3, 2, 8, STATIONS), F32),
        ]
        + [pltpu.VMEM((STATIONS, 256), F32)] * 8,
        compiler_params=pltpu.CompilerParams(vmem_limit_bytes=24 * 2**20),
        name="pairs",
    )(index, recv, *prepared)


def steering_phases(positions, directions, channel):
    order = positions.reshape(BLOCKS, SPB, 2).transpose(2, 1, 0).reshape(2, STATIONS)
    delays = order[0][None, :] * directions[:, 0][:, None] + order[1][None, :] * directions[:, 1][:, None]
    scaled = 2.0 * math.pi * (1.0 + channel.astype(F32) / F)
    phases = scaled * delays
    return jnp.cos(phases), jnp.sin(phases)


def body(voltages, station_gains, positions, directions, weights, baseline_flags):
    chan_index = lax.axis_index("chan")
    stn_index = lax.axis_index("stn")
    index = jnp.reshape(chan_index, (1,)).astype(jnp.int32)
    channel = chan_index * BLOCKS + stn_index
    volts = arrange(voltages)
    payload = make_spectra(index, volts, station_gains[:, 0, :], baseline_flags)
    recv = lax.all_to_all(
        payload.reshape(CW, 4, 128), ("chan", "stn"), split_axis=0, concat_axis=0, tiled=True
    )
    cos, sin = steering_phases(positions, directions, channel)
    steps = make_steps(index, recv.reshape(4 * CW, 128), *make_steering(cos, sin, weights))
    return lax.all_to_all(steps.reshape(BLOCKS, 1, 128), "stn", split_axis=0, concat_axis=0, tiled=True)


def solution(mesh):
    in_specs = (P("stn", "chan", None, None), P("chan", "stn", None), P(), P(), P(), P("stn", None))
    out_specs = P("chan", "stn", None)
    return jax.shard_map(body, mesh=mesh, in_specs=in_specs, out_specs=out_specs, check_vma=False)
```

```python
import math

import jax
import jax.numpy as jnp
import numpy as np
from jax import lax
from jax.experimental import pallas as pl
from jax.experimental.pallas import tpu as pltpu
from jax.sharding import PartitionSpec as P

F = 4096
CW = 512
FRAME = 8192
TAPS = 16
STATIONS = 512
NFRAMES = 16
SOURCES = 32
BLOCKS = 16
SPB = 32
FRAMES_IN = NFRAMES + TAPS - 1
CHUNKS = 8
CHUNK = 16
ROWS = 256
BF = jnp.bfloat16
F32 = jnp.float32


def split_np(values):
    hi = values.astype(jnp.bfloat16)
    lo = (values - hi.astype(np.float64)).astype(jnp.bfloat16)
    return hi, lo


def filter_tables():
    n = np.arange(TAPS * FRAME, dtype=np.float64)
    q = (n + 0.5 - TAPS * FRAME / 2) / FRAME
    window = np.sin(np.pi * q) / (np.pi * q) * (0.5 - 0.5 * np.cos(2 * np.pi * n / (TAPS * FRAME)))
    window = window.astype(np.float32).reshape(TAPS, 64, 128)
    window = np.repeat(window, 2, axis=1).reshape(TAPS, CHUNKS, 16, 128).transpose(1, 0, 2, 3)
    j = np.arange(64)[:, None]
    k = np.arange(64)[None, :]
    angle = 2 * np.pi * (k * j % 64) / 64
    first = np.stack([np.cos(angle), -np.sin(angle)])
    first = np.einsum("cjk,st->jsctk", first, np.eye(2)).reshape(128, 256)
    hi, lo = split_np(first)
    first = np.concatenate([hi, hi, lo], axis=0)
    m = np.arange(128)[:, None]
    angle = 2 * np.pi * (k * m % 8192) / 8192
    turn = np.stack([np.cos(angle), np.sin(angle)])
    turn = np.concatenate([turn, turn], axis=2).astype(np.float32)
    b = np.arange(8)[:, None]
    m = np.arange(128)[None, :]
    angle = 2 * np.pi * (b * m % 128) / 128
    c = np.cos(angle) / math.sqrt(FRAME)
    s = np.sin(angle) / math.sqrt(FRAME)
    to_re = np.concatenate([c, s], axis=1)
    to_im = np.concatenate([-s, c], axis=1)
    second = np.stack([to_re, to_im], axis=1).reshape(16, 256)
    second = np.concatenate(split_np(second), axis=0)
    return window, first, turn, second


def split2(x):
    hi = x.astype(BF)
    return hi, (x - hi.astype(F32)).astype(BF)


def dot(a, b):
    return lax.dot_general(a, b, (((1,), (0,)), ((), ())), preferred_element_type=F32)


def dot_nt(a, b):
    return lax.dot_general(a, b, (((1,), (1,)), ((), ())), preferred_element_type=F32)


def iota(shape, dim):
    return lax.broadcasted_iota(jnp.int32, shape, dim)


def sine_cosine(x):
    turns = jnp.floor(x * (2.0 / math.pi) + 0.5)
    r = x - turns * 1.5703125
    r = r - turns * 4.837512969970703125e-4
    r = r - turns * 7.54978995489188216e-8
    z = r * r
    sine = ((-1.9515295891e-4 * z + 8.3321608736e-3) * z - 1.6666654611e-1) * z * r + r
    cosine = ((2.443315711809948e-5 * z - 1.388731625493765e-3) * z + 4.166664568298827e-2) * z * z - 0.5 * z + 1.0
    quarter = turns.astype(jnp.int32) & 3
    odd = (quarter & 1) == 1
    sin = jnp.where(odd, cosine, sine)
    cos = jnp.where(odd, sine, cosine)
    sin = jnp.where(quarter >= 2, -sin, sin)
    cos = jnp.where((quarter == 1) | (quarter == 2), -cos, cos)
    return sin, cos


def prepare_steering(channel, position, columns, near_e, steer_ref, turned_ref):
    east, north = position[0:1, :], position[1:2, :]
    delays = columns[0:SOURCES, 0:1] * east + columns[0:SOURCES, 1:2] * north
    scaled = 2.0 * math.pi * (1.0 + channel.astype(F32) / F)
    sin, cos = sine_cosine(scaled * delays)
    parts = []
    for p in range(2):
        weight = columns[0:SOURCES, 2 + p : 3 + p]
        parts += [(cos * weight).astype(BF), (-sin * weight).astype(BF)]
    source, target = iota((STATIONS, STATIONS), 0), iota((1, STATIONS), 1)
    wanted = (target & 15) * SPB + lax.shift_right_logical(target, 4)
    ordered = dot(jnp.concatenate(parts, axis=0), jnp.where(source == wanted, 1.0, 0.0).astype(BF))
    steer, turned = [], []
    for p in range(2):
        re, im = ordered[p * 64 : p * 64 + 32], ordered[p * 64 + 32 : p * 64 + 64]
        steer += [re, im]
        turned += [-im, re]
        near_e[p, 0] = jnp.concatenate([re, im, re, im], axis=0).astype(BF)
        near_e[p, 1] = jnp.concatenate([-im, re, -im, re], axis=0).astype(BF)
    steer_ref[...] = jnp.concatenate(steer, axis=0).T
    turned_ref[...] = jnp.concatenate(turned, axis=0).T


def prepare_matrices(own_ref, row_ref, wide_ref, code_ref, move_ref):
    station = iota((STATIONS, 128), 0)
    lane = iota((STATIONS, 128), 1)
    place, block = lax.shift_right_logical(station, 4), station & 15
    own_ref[...] = jnp.where(lax.shift_right_logical(lane & 63, 1) == place, 1.0, 0.0)
    row_ref[...] = jnp.where(block == lane, 1.0, 0.0).astype(BF)
    source = iota((128, 256), 0)
    target = iota((128, 256), 1)
    fits = ((source & 1) == (lax.shift_right_logical(target, 6) & 1)) & (
        lax.shift_right_logical(source, 6) == lax.shift_right_logical(target, 7)
    )
    wide_ref[...] = jnp.where(fits, 1.0, 0.0).astype(BF)
    code = iota((16, 128), 0)
    lane = iota((16, 128), 1)
    fits = ((lane & 1) == (code & 1)) & (lax.shift_right_logical(lane, 6) == lax.shift_right_logical(code, 1))
    code_ref[...] = jnp.where(fits, 1.0, 0.0).astype(BF)
    for n in range(4):
        column = (n // 2) * 64 + place * 2 + (n % 2)
        move_ref[n] = jnp.where(iota((STATIONS, 128), 1) == column, 1.0, 0.0).astype(BF)


def spectra_kernel(
    index_ref,
    volt_ref,
    win_ref,
    first_ref,
    turn_ref,
    second_ref,
    gain_ref,
    flag_ref,
    position_ref,
    direction_ref,
    weight_ref,
    out_ref,
    near_e,
    steer_ref,
    turned_ref,
    own_ref,
    row_ref,
    wide_ref,
    code_ref,
    move_ref,
    volts,
    window,
    first,
    turn,
    second,
    gain,
    flag,
    position,
    direction,
    weight,
    table,
    pick,
    fold,
    left,
    section,
    high,
    low,
    gathered,
    part,
    sems,
    late,
):
    def volt_copy(step):
        rows = pl.ds(pl.multiple_of(step * 16, 16), 16)
        return pltpu.make_async_copy(volt_ref.at[:, rows, :], volts.at[step], sems.at[0, step])

    def window_copy(step):
        return pltpu.make_async_copy(win_ref.at[step], window.at[step], sems.at[1, step])

    others = [
        pltpu.make_async_copy(source, target, late.at[n])
        for n, (source, target) in enumerate(
            ((first_ref, first), (turn_ref, turn), (second_ref, second), (gain_ref, gain), (flag_ref, flag))
        )
    ]
    small = [
        pltpu.make_async_copy(position_ref, position, late.at[5]),
        pltpu.make_async_copy(direction_ref, direction, late.at[6]),
        pltpu.make_async_copy(weight_ref, weight, late.at[7]),
    ]
    table[...] = jnp.zeros((8, 128), F32)
    for copy in small:
        copy.start()
    for step in range(CHUNKS):
        volt_copy(step).start()
        window_copy(step).start()
    for copy in others:
        copy.start()

    channel = index_ref[0]
    index = channel // BLOCKS
    place = (iota((1, 384), 1) + 64 * (index // 4)) & (STATIONS - 1)
    wanted = (place & 15) * SPB + lax.shift_right_logical(place, 4)
    pick[...] = jnp.where(iota((STATIONS, 384), 0) == wanted, 1.0, 0.0).astype(BF)

    prepare_matrices(own_ref, row_ref, wide_ref, code_ref, move_ref)

    def chunk(step, carry):
        volt_copy(step).wait()
        window_copy(step).wait()
        x = volts[step].astype(F32)
        acc = x[0:NFRAMES] * window[step, 0][None]
        for tap in range(1, TAPS):
            acc = acc + x[tap : tap + NFRAMES] * window[step, tap][None]
        fold[:, pl.ds(pl.multiple_of(step * 16, 16), 16), :] = acc
        return carry

    lax.fori_loop(0, CHUNKS, chunk, 0)
    for copy in small:
        copy.wait()
    table[0:2, 0:SOURCES] = direction[...]
    table[2:4, 0:SOURCES] = weight[...]
    prepare_steering(channel, position[...], table[...].T, near_e, steer_ref, turned_ref)
    for copy in others:
        copy.wait()

    turn_cos = turn[0]
    turn_sin = turn[1]
    for t in range(NFRAMES):
        hi, lo = split2(fold[t].T)
        rows = slice(t * 128, t * 128 + 128)
        left[rows, 0:128] = hi
        left[rows, 128:256] = lo
    for group in range(4):
        rows = slice(group * 512, group * 512 + 512)
        section[rows, :] = dot(left[rows, :], first[0:256]) + dot(left[rows, 0:128], first[256:384])
    for t in range(NFRAMES):
        rows = slice(t * 128, t * 128 + 128)
        re = section[rows, 0:128]
        im = section[rows, 128:256]
        for part_id, value in enumerate((re * turn_cos + im * turn_sin, im * turn_cos - re * turn_sin)):
            hi, lo = split2(value)
            place = slice(part_id * 128, part_id * 128 + 128)
            high[place, rows] = hi
            low[place, rows] = lo
    main = dot(second[...], high[...])
    rest = dot(second[0:16], low[...])
    value = main[0:16] + (main[16:32] + rest)
    for t in range(NFRAMES):
        gathered[pl.ds(t, 16, stride=16), :] = value[:, t * 128 : t * 128 + 128]
    total = gathered[...].T

    flags = jnp.broadcast_to(flag[pl.ds(index, 1), :].astype(F32), (8, STATIONS)).astype(BF)
    row = dot(flags, pick[...])[0:1]

    for b in range(8):
        lanes = [
            total[0:64, b * 32 : b * 32 + 32],
            total[64:128, b * 32 : b * 32 + 32],
            jnp.broadcast_to(row[:, 0:64], (64, 64)),
        ]
        part[pl.ds(b * 256, 64, stride=4), :] = jnp.concatenate(lanes, axis=1)
    part[pl.ds(1, 512, stride=4), :] = jnp.broadcast_to(row[:, 64:192], (512, 128))
    part[pl.ds(2, 512, stride=4), :] = jnp.broadcast_to(row[:, 192:320], (512, 128))
    gains = gain[...].astype(F32)
    for i in range(32):
        part[pl.ds(i * 64 + 3, 16, stride=4), :] = gains
    out_ref[...] = part[...].astype(BF)


def pair_kernel(
    index_ref,
    recv_ref,
    near_e,
    steer_ref,
    turned_ref,
    own_ref,
    row_ref,
    wide_ref,
    code_ref,
    move_ref,
    out_ref,
    part,
    near_x,
    far_x,
    far_e,
    brought,
    usable,
    acc,
    *products,
):
    part[...] = recv_ref[...].astype(F32)
    first = part[pl.ds(0, 512, stride=4), :]
    index = index_ref[0] // BLOCKS

    sent = jnp.concatenate(
        [
            first[:, 64:128],
            part[pl.ds(1, 512, stride=4), :],
            part[pl.ds(2, 512, stride=4), :],
        ],
        axis=1,
    )
    empty = jnp.zeros((64, 64), F32)
    for a in range(8):
        pieces = []
        for b in range(8):
            d = (b - a) % 8
            pieces.append(sent[a * 64 : a * 64 + 64, d * 64 : d * 64 + 64] if d <= 4 else empty)
        brought[pl.ds(a * 64, 64), :] = jnp.concatenate(pieces, axis=1)
    turned = brought[...].T
    low = iota((64, 128), 1) < 64
    for a in range(8):
        rows = slice(a * 64, a * 64 + 64)
        for b in range(0, 8, 2):
            cols = slice(b * 64, b * 64 + 128)
            direct, back = brought[rows, cols], turned[rows, cols]
            known = [(n - a) % 8 <= 4 for n in (b, b + 1)]
            if known == [True, True]:
                both = direct
            elif known == [False, False]:
                both = back
            else:
                both = jnp.where(low == known[0], direct, back)
            if a // 2 == b // 2:
                both = jnp.where(iota((64, 128), 0) + (a - b) * 64 == iota((64, 128), 1), 0.0, both)
            usable[rows, cols] = both

    xt = first.T
    for p in range(2):
        own = xt[p * 32 : p * 32 + 32]
        near_x[p, 0] = own.astype(BF)
        near_x[p, 1] = jnp.concatenate([own[16:32], -own[0:16]], axis=0).astype(BF)
        far_x[p] = first[:, p * 32 : p * 32 + 32].astype(BF)

    gains = part[pl.ds(index * 64 + 3, 16, stride=4), :].astype(BF)
    gains = jnp.concatenate([gains, jnp.zeros((112, 128), BF)], axis=0)
    spread = (dot(row_ref[...], gains) * own_ref[...]).astype(BF)
    wide = dot(spread, wide_ref[...])
    scaled = wide[:, 0:128] * steer_ref[...] + wide[:, 128:256] * turned_ref[...]
    for q in range(2):
        hi, lo = split2(scaled[:, q * 64 : q * 64 + 64])
        far_e[q] = jnp.concatenate([hi, lo], axis=1)
    near_gain = dot_nt(code_ref[...], spread)

    blocks = [(p, half, q) for p in range(2) for half in range(2) for q in range(2)]
    sums = {}
    for n in range(len(blocks) + 1):
        for r in range(0, STATIONS, ROWS):
            rows = slice(r, r + ROWS)
            if n < len(blocks):
                p, half, q = blocks[n]
                cols = slice(half * 256, half * 256 + 256)
                vr, vi, ar, ai = products[4 * (n % 2) : 4 * (n % 2) + 4]
                vr[rows, :] = dot(far_x[q, rows], near_x[p, 0, :, cols])
                vi[rows, :] = dot(far_x[q, rows], near_x[p, 1, :, cols])
                ar[rows, :] = dot(far_e[q, rows], near_e[p, 0, :, cols])
                ai[rows, :] = dot(far_e[q, rows], near_e[p, 1, :, cols])
            if n > 0:
                p, half, q = blocks[n - 1]
                cols = slice(half * 256, half * 256 + 256)
                vr, vi, ar, ai = products[4 * ((n - 1) % 2) : 4 * ((n - 1) % 2) + 4]
                total = sums.get((p, half), [jnp.zeros((8, 256), F32)] * 3)
                for c in range(r, r + ROWS, CHUNK):
                    some = slice(c, c + CHUNK)
                    mask = usable[some, cols]
                    ur, ui = mask * ar[some, :], mask * ai[some, :]
                    xr, xi = vr[some, :], vi[some, :]
                    terms = (xr * ur - xi * ui, xr * ui + xi * ur, ur * ur + ui * ui)
                    total = [s + jnp.sum(t.reshape(CHUNK // 8, 8, 256), axis=0) for s, t in zip(total, terms)]
                sums[p, half] = total
    for (p, half), total in sums.items():
        for n in range(3):
            acc[n, p, :, half * 256 : half * 256 + 256] = total[n]

    steps = []
    for part_id in range(2):
        for p in range(2):
            weight_sum = jnp.sum(acc[2, p], axis=0, keepdims=True)
            moment = jnp.sum(acc[part_id, p], axis=0, keepdims=True) * (1.0 / NFRAMES)
            own = near_gain[part_id * 2 + p : part_id * 2 + p + 1]
            steps.append((moment - own * weight_sum) / (1.0 + weight_sum))

    mine = (iota((16, 512), 1) & 15) == iota((16, 512), 0)
    placed = jnp.zeros((48, 128), F32)
    for n, value in enumerate(steps):
        value = jnp.where(mine, jnp.broadcast_to(value, (16, 512)), 0.0)
        hi = value.astype(BF)
        rest = value - hi.astype(F32)
        mid = rest.astype(BF)
        low = (rest - mid.astype(F32)).astype(BF)
        placed = placed + dot(jnp.concatenate([hi, mid, low], axis=0), move_ref[n])
    out_ref[...] = placed[0:16] + (placed[16:32] + placed[32:48])


def whole():
    return pl.BlockSpec(memory_space=pltpu.VMEM)


def held(x):
    return pltpu.with_memory_space_constraint(x, pltpu.HBM)


def anywhere():
    return pl.BlockSpec(memory_space=pltpu.HBM)


def make_spectra(channel, volts, gains, flags, positions, directions, weights):
    window, first, turn, second = filter_tables()
    operands = [volts, jnp.asarray(window), jnp.asarray(first), jnp.asarray(turn), jnp.asarray(second), gains, flags]
    operands = [held(x) for x in operands + [positions.T, directions.T, weights.T]]
    return pl.pallas_call(
        spectra_kernel,
        out_shape=(
            pltpu.VMEM((4 * CW, 128), BF),
            pltpu.VMEM((2, 2, 128, STATIONS), BF),
            pltpu.VMEM((STATIONS, 128), F32),
            pltpu.VMEM((STATIONS, 128), F32),
            pltpu.VMEM((STATIONS, 128), F32),
            pltpu.VMEM((STATIONS, 128), BF),
            pltpu.VMEM((128, 256), BF),
            pltpu.VMEM((16, 128), BF),
            pltpu.VMEM((4, STATIONS, 128), BF),
        ),
        in_specs=[pl.BlockSpec(memory_space=pltpu.SMEM)] + [anywhere()] * 10,
        out_specs=(whole(),) * 9,
        scratch_shapes=[
            pltpu.VMEM((CHUNKS, FRAMES_IN, 16, 128), BF),
            pltpu.VMEM((CHUNKS, TAPS, 16, 128), F32),
            pltpu.VMEM((384, 256), BF),
            pltpu.VMEM((2, 128, 128), F32),
            pltpu.VMEM((32, 256), BF),
            pltpu.VMEM((BLOCKS, 128), BF),
            pltpu.VMEM((SPB, STATIONS), jnp.int32),
            pltpu.VMEM((2, STATIONS), F32),
            pltpu.VMEM((2, SOURCES), F32),
            pltpu.VMEM((2, SOURCES), F32),
            pltpu.VMEM((8, 128), F32),
            pltpu.VMEM((STATIONS, 384), BF),
            pltpu.VMEM((NFRAMES, 128, 128), F32),
            pltpu.VMEM((NFRAMES * 128, 256), BF),
            pltpu.VMEM((NFRAMES * 128, 256), F32),
            pltpu.VMEM((256, NFRAMES * 128), BF),
            pltpu.VMEM((256, NFRAMES * 128), BF),
            pltpu.VMEM((256, 128), F32),
            pltpu.VMEM((4 * CW, 128), F32),
            pltpu.SemaphoreType.DMA((2, CHUNKS)),
            pltpu.SemaphoreType.DMA((8,)),
        ],
        compiler_params=pltpu.CompilerParams(vmem_limit_bytes=28 * 2**20),
        name="spectra",
    )(channel, *operands)


def arrange(voltages):
    rows = voltages.reshape(2, FRAMES_IN * 64, 128).transpose(1, 0, 2)
    return rows.reshape(FRAMES_IN, 128, 128)


def make_steps(index, recv, *prepared):
    return pl.pallas_call(
        pair_kernel,
        out_shape=jax.ShapeDtypeStruct((BLOCKS, 128), F32),
        in_specs=[pl.BlockSpec(memory_space=pltpu.SMEM)] + [whole()] * 9,
        out_specs=whole(),
        scratch_shapes=[
            pltpu.VMEM((4 * STATIONS, 128), F32),
            pltpu.VMEM((2, 2, 32, STATIONS), BF),
            pltpu.VMEM((2, STATIONS, 32), BF),
            pltpu.VMEM((2, STATIONS, 128), BF),
            pltpu.VMEM((STATIONS, STATIONS), F32),
            pltpu.VMEM((STATIONS, STATIONS), F32),
            pltpu.VMEM((3, 2, 8, STATIONS), F32),
        ]
        + [pltpu.VMEM((STATIONS, 256), F32)] * 8,
        compiler_params=pltpu.CompilerParams(vmem_limit_bytes=24 * 2**20),
        name="pairs",
    )(index, recv, *prepared)


def body(voltages, station_gains, positions, directions, weights, baseline_flags):
    channel = jnp.reshape(lax.axis_index("chan") * BLOCKS + lax.axis_index("stn"), (1,)).astype(jnp.int32)
    payload, *prepared = make_spectra(
        channel, arrange(voltages), station_gains[:, 0, :], baseline_flags, positions, directions, weights
    )
    recv = lax.all_to_all(
        payload.reshape(CW, 4, 128), ("chan", "stn"), split_axis=0, concat_axis=0, tiled=True
    )
    steps = make_steps(channel, recv.reshape(4 * CW, 128), *prepared)
    return lax.all_to_all(steps.reshape(BLOCKS, 1, 128), "stn", split_axis=0, concat_axis=0, tiled=True)


def solution(mesh):
    in_specs = (P("stn", "chan", None, None), P("chan", "stn", None), P(), P(), P(), P("stn", None))
    out_specs = P("chan", "stn", None)
    return jax.shard_map(body, mesh=mesh, in_specs=in_specs, out_specs=out_specs, check_vma=False)
```

```python
import math

import jax
import jax.numpy as jnp
import numpy as np
from jax import lax
from jax.experimental import pallas as pl
from jax.experimental.pallas import tpu as pltpu
from jax.sharding import Mesh
from jax.sharding import PartitionSpec as P

F = 4096
CW = 512
FRAME = 8192
TAPS = 16
STATIONS = 512
NFRAMES = 16
SOURCES = 32
BLOCKS = 16
SPB = 32
FRAMES_IN = NFRAMES + TAPS - 1
CHUNKS = 8
CHUNK = 16
ROWS = 256
CHAN = ("y", "z_hi", "core")
STN = ("x", "z_lo")
ORDER = ("core", "y", "z_hi") + STN
BF = jnp.bfloat16
F32 = jnp.float32


def split_np(values):
    hi = values.astype(jnp.bfloat16)
    lo = (values - hi.astype(np.float64)).astype(jnp.bfloat16)
    return hi, lo


def filter_tables():
    n = np.arange(TAPS * FRAME, dtype=np.float64)
    q = (n + 0.5 - TAPS * FRAME / 2) / FRAME
    window = np.sin(np.pi * q) / (np.pi * q) * (0.5 - 0.5 * np.cos(2 * np.pi * n / (TAPS * FRAME)))
    window = window.astype(np.float32).reshape(TAPS, 64, 128)
    window = np.repeat(window, 2, axis=1).reshape(TAPS, CHUNKS, 16, 128).transpose(1, 0, 2, 3)
    j = np.arange(64)[:, None]
    k = np.arange(64)[None, :]
    angle = 2 * np.pi * (k * j % 64) / 64
    first = np.stack([np.cos(angle), -np.sin(angle)])
    first = np.einsum("cjk,st->jsctk", first, np.eye(2)).reshape(128, 256)
    hi, lo = split_np(first)
    first = np.concatenate([hi, hi, lo], axis=0)
    m = np.arange(128)[:, None]
    angle = 2 * np.pi * (k * m % 8192) / 8192
    turn = np.stack([np.cos(angle), np.sin(angle)])
    turn = np.concatenate([turn, turn], axis=2).astype(np.float32)
    b = np.arange(8)[:, None]
    m = np.arange(128)[None, :]
    angle = 2 * np.pi * (b * m % 128) / 128
    c = np.cos(angle) / math.sqrt(FRAME)
    s = np.sin(angle) / math.sqrt(FRAME)
    to_re = np.concatenate([c, s], axis=1)
    to_im = np.concatenate([-s, c], axis=1)
    second = np.stack([to_re, to_im], axis=1).reshape(16, 256)
    second = np.concatenate(split_np(second), axis=0)
    return window, first, turn, second


def split2(x):
    hi = x.astype(BF)
    return hi, (x - hi.astype(F32)).astype(BF)


def dot(a, b):
    return lax.dot_general(a, b, (((1,), (0,)), ((), ())), preferred_element_type=F32)


def dot_nt(a, b):
    return lax.dot_general(a, b, (((1,), (1,)), ((), ())), preferred_element_type=F32)


def iota(shape, dim):
    return lax.broadcasted_iota(jnp.int32, shape, dim)


def place_of(n):
    return (lax.shift_right_logical(n, 5) & 7) * 4 + (lax.shift_right_logical(n, 4) & 1) * 2 + lax.shift_right_logical(n, 8)


def number_of(channel):
    group = channel // BLOCKS
    return (group % 2) * 256 + (group // 4) * 32 + ((group // 2) % 2) * 16 + channel % BLOCKS


def sine_cosine(x):
    turns = jnp.floor(x * (2.0 / math.pi) + 0.5)
    r = x - turns * 1.5703125
    r = r - turns * 4.837512969970703125e-4
    r = r - turns * 7.54978995489188216e-8
    z = r * r
    sine = ((-1.9515295891e-4 * z + 8.3321608736e-3) * z - 1.6666654611e-1) * z * r + r
    cosine = ((2.443315711809948e-5 * z - 1.388731625493765e-3) * z + 4.166664568298827e-2) * z * z - 0.5 * z + 1.0
    quarter = turns.astype(jnp.int32) & 3
    odd = (quarter & 1) == 1
    sin = jnp.where(odd, cosine, sine)
    cos = jnp.where(odd, sine, cosine)
    sin = jnp.where(quarter >= 2, -sin, sin)
    cos = jnp.where((quarter == 1) | (quarter == 2), -cos, cos)
    return sin, cos


def prepare_steering(channel, position, columns, near_e, steer_ref, turned_ref):
    east, north = position[0:1, :], position[1:2, :]
    delays = columns[0:SOURCES, 0:1] * east + columns[0:SOURCES, 1:2] * north
    scaled = 2.0 * math.pi * (1.0 + channel.astype(F32) / F)
    sin, cos = sine_cosine(scaled * delays)
    parts = []
    for p in range(2):
        weight = columns[0:SOURCES, 2 + p : 3 + p]
        parts += [(cos * weight).astype(BF), (-sin * weight).astype(BF)]
    source, target = iota((STATIONS, STATIONS), 0), iota((1, STATIONS), 1)
    wanted = (target & 15) * SPB + place_of(target)
    ordered = dot(jnp.concatenate(parts, axis=0), jnp.where(source == wanted, 1.0, 0.0).astype(BF))
    steer, turned = [], []
    for p in range(2):
        re, im = ordered[p * 64 : p * 64 + 32], ordered[p * 64 + 32 : p * 64 + 64]
        steer += [re, im]
        turned += [-im, re]
        near_e[p, 0] = jnp.concatenate([re, im, re, im], axis=0).astype(BF)
        near_e[p, 1] = jnp.concatenate([-im, re, -im, re], axis=0).astype(BF)
    steer_ref[...] = jnp.concatenate(steer, axis=0).T
    turned_ref[...] = jnp.concatenate(turned, axis=0).T


def prepare_matrices(own_ref, row_ref, wide_ref, code_ref, move_ref):
    station = iota((STATIONS, 128), 0)
    lane = iota((STATIONS, 128), 1)
    place, block = place_of(station), station & 15
    own_ref[...] = jnp.where(lax.shift_right_logical(lane & 63, 1) == place, 1.0, 0.0)
    row_ref[...] = jnp.where(block == lane, 1.0, 0.0).astype(BF)
    source = iota((128, 256), 0)
    target = iota((128, 256), 1)
    fits = ((source & 1) == (lax.shift_right_logical(target, 6) & 1)) & (
        lax.shift_right_logical(source, 6) == lax.shift_right_logical(target, 7)
    )
    wide_ref[...] = jnp.where(fits, 1.0, 0.0).astype(BF)
    code = iota((16, 128), 0)
    lane = iota((16, 128), 1)
    fits = ((lane & 1) == (code & 1)) & (lax.shift_right_logical(lane, 6) == lax.shift_right_logical(code, 1))
    code_ref[...] = jnp.where(fits, 1.0, 0.0).astype(BF)
    for n in range(4):
        column = (n // 2) * 64 + place * 2 + (n % 2)
        move_ref[n] = jnp.where(iota((STATIONS, 128), 1) == column, 1.0, 0.0).astype(BF)


def spectra_kernel(
    index_ref,
    volt_ref,
    win_ref,
    first_ref,
    turn_ref,
    second_ref,
    gain_ref,
    flag_ref,
    position_ref,
    direction_ref,
    weight_ref,
    out_ref,
    near_e,
    steer_ref,
    turned_ref,
    own_ref,
    row_ref,
    wide_ref,
    code_ref,
    move_ref,
    volts,
    window,
    first,
    turn,
    second,
    gain,
    flag,
    position,
    direction,
    weight,
    table,
    pick,
    fold,
    left,
    section,
    high,
    low,
    gathered,
    part,
    sems,
    late,
):
    def volt_copy(step):
        rows = pl.ds(pl.multiple_of(step * 16, 16), 16)
        return pltpu.make_async_copy(volt_ref.at[:, rows, :], volts.at[step], sems.at[0, step])

    def window_copy(step):
        return pltpu.make_async_copy(win_ref.at[step], window.at[step], sems.at[1, step])

    others = [
        pltpu.make_async_copy(source, target, late.at[n])
        for n, (source, target) in enumerate(
            ((first_ref, first), (turn_ref, turn), (second_ref, second), (gain_ref, gain), (flag_ref, flag))
        )
    ]
    small = [
        pltpu.make_async_copy(position_ref, position, late.at[5]),
        pltpu.make_async_copy(direction_ref, direction, late.at[6]),
        pltpu.make_async_copy(weight_ref, weight, late.at[7]),
    ]
    table[...] = jnp.zeros((8, 128), F32)
    for copy in small:
        copy.start()
    for step in range(CHUNKS):
        volt_copy(step).start()
        window_copy(step).start()
    for copy in others:
        copy.start()

    channel = index_ref[0]
    index = channel // BLOCKS
    place = (iota((1, 384), 1) + 64 * (number_of(channel) // 64)) & (STATIONS - 1)
    wanted = (place & 15) * SPB + place_of(place)
    pick[...] = jnp.where(iota((STATIONS, 384), 0) == wanted, 1.0, 0.0).astype(BF)

    prepare_matrices(own_ref, row_ref, wide_ref, code_ref, move_ref)

    def chunk(step, carry):
        volt_copy(step).wait()
        window_copy(step).wait()
        x = volts[step].astype(F32)
        acc = x[0:NFRAMES] * window[step, 0][None]
        for tap in range(1, TAPS):
            acc = acc + x[tap : tap + NFRAMES] * window[step, tap][None]
        fold[:, pl.ds(pl.multiple_of(step * 16, 16), 16), :] = acc
        return carry

    lax.fori_loop(0, CHUNKS, chunk, 0)
    for copy in small:
        copy.wait()
    table[0:2, 0:SOURCES] = direction[...]
    table[2:4, 0:SOURCES] = weight[...]
    prepare_steering(channel, position[...], table[...].T, near_e, steer_ref, turned_ref)
    for copy in others:
        copy.wait()

    turn_cos = turn[0]
    turn_sin = turn[1]
    for t in range(NFRAMES):
        hi, lo = split2(fold[t].T)
        rows = slice(t * 128, t * 128 + 128)
        left[rows, 0:128] = hi
        left[rows, 128:256] = lo
    for group in range(4):
        rows = slice(group * 512, group * 512 + 512)
        section[rows, :] = dot(left[rows, :], first[0:256]) + dot(left[rows, 0:128], first[256:384])
    for t in range(NFRAMES):
        rows = slice(t * 128, t * 128 + 128)
        re = section[rows, 0:128]
        im = section[rows, 128:256]
        for part_id, value in enumerate((re * turn_cos + im * turn_sin, im * turn_cos - re * turn_sin)):
            hi, lo = split2(value)
            place = slice(part_id * 128, part_id * 128 + 128)
            high[place, rows] = hi
            low[place, rows] = lo
    main = dot(second[...], high[...])
    rest = dot(second[0:16], low[...])
    value = main[0:16] + (main[16:32] + rest)
    for t in range(NFRAMES):
        gathered[pl.ds(t, 16, stride=16), :] = value[:, t * 128 : t * 128 + 128]
    total = gathered[...].T

    flags = jnp.broadcast_to(flag[pl.ds(index, 1), :].astype(F32), (8, STATIONS)).astype(BF)
    row = dot(flags, pick[...])[0:1]

    for b in range(8):
        lanes = [
            total[0:64, b * 32 : b * 32 + 32],
            total[64:128, b * 32 : b * 32 + 32],
            jnp.broadcast_to(row[:, 0:64], (64, 64)),
        ]
        rows = jnp.concatenate(lanes, axis=1)
        for n in range(4):
            target = (n % 2) * 256 + b * 32 + (n // 2) * 16
            part[pl.ds(target * 4, 16, stride=4), :] = rows[n * 16 : n * 16 + 16]
    part[pl.ds(1, 512, stride=4), :] = jnp.broadcast_to(row[:, 64:192], (512, 128))
    part[pl.ds(2, 512, stride=4), :] = jnp.broadcast_to(row[:, 192:320], (512, 128))
    gains = gain[...].astype(F32)
    for i in range(32):
        part[pl.ds(i * 64 + 3, 16, stride=4), :] = gains
    out_ref[...] = part[...].astype(BF)


def pair_kernel(
    index_ref,
    recv_ref,
    near_e,
    steer_ref,
    turned_ref,
    own_ref,
    row_ref,
    wide_ref,
    code_ref,
    move_ref,
    out_ref,
    part,
    near_x,
    far_x,
    far_e,
    brought,
    usable,
    acc,
    *products,
):
    part[...] = recv_ref[...].astype(F32)
    first = part[pl.ds(0, 512, stride=4), :]
    channel = index_ref[0]

    sent = jnp.concatenate(
        [
            first[:, 64:128],
            part[pl.ds(1, 512, stride=4), :],
            part[pl.ds(2, 512, stride=4), :],
        ],
        axis=1,
    )
    empty = jnp.zeros((64, 64), F32)
    for a in range(8):
        pieces = []
        for b in range(8):
            d = (b - a) % 8
            pieces.append(sent[a * 64 : a * 64 + 64, d * 64 : d * 64 + 64] if d <= 4 else empty)
        brought[pl.ds(a * 64, 64), :] = jnp.concatenate(pieces, axis=1)
    turned = brought[...].T
    low = iota((64, 128), 1) < 64
    for a in range(8):
        rows = slice(a * 64, a * 64 + 64)
        for b in range(0, 8, 2):
            cols = slice(b * 64, b * 64 + 128)
            direct, back = brought[rows, cols], turned[rows, cols]
            known = [(n - a) % 8 <= 4 for n in (b, b + 1)]
            if known == [True, True]:
                both = direct
            elif known == [False, False]:
                both = back
            else:
                both = jnp.where(low == known[0], direct, back)
            if a // 2 == b // 2:
                both = jnp.where(iota((64, 128), 0) + (a - b) * 64 == iota((64, 128), 1), 0.0, both)
            usable[rows, cols] = both

    xt = first.T
    for p in range(2):
        own = xt[p * 32 : p * 32 + 32]
        near_x[p, 0] = own.astype(BF)
        near_x[p, 1] = jnp.concatenate([own[16:32], -own[0:16]], axis=0).astype(BF)
        far_x[p] = first[:, p * 32 : p * 32 + 32].astype(BF)

    gains = part[pl.ds((number_of(channel) - channel % BLOCKS) * 4 + 3, 16, stride=4), :].astype(BF)
    gains = jnp.concatenate([gains, jnp.zeros((112, 128), BF)], axis=0)
    spread = (dot(row_ref[...], gains) * own_ref[...]).astype(BF)
    wide = dot(spread, wide_ref[...])
    scaled = wide[:, 0:128] * steer_ref[...] + wide[:, 128:256] * turned_ref[...]
    for q in range(2):
        hi, lo = split2(scaled[:, q * 64 : q * 64 + 64])
        far_e[q] = jnp.concatenate([hi, lo], axis=1)
    near_gain = dot_nt(code_ref[...], spread)

    blocks = [(p, half, q) for p in range(2) for half in range(2) for q in range(2)]
    sums = {}
    for n in range(len(blocks) + 1):
        for r in range(0, STATIONS, ROWS):
            rows = slice(r, r + ROWS)
            if n < len(blocks):
                p, half, q = blocks[n]
                cols = slice(half * 256, half * 256 + 256)
                vr, vi, ar, ai = products[4 * (n % 2) : 4 * (n % 2) + 4]
                vr[rows, :] = dot(far_x[q, rows], near_x[p, 0, :, cols])
                vi[rows, :] = dot(far_x[q, rows], near_x[p, 1, :, cols])
                ar[rows, :] = dot(far_e[q, rows], near_e[p, 0, :, cols])
                ai[rows, :] = dot(far_e[q, rows], near_e[p, 1, :, cols])
            if n > 0:
                p, half, q = blocks[n - 1]
                cols = slice(half * 256, half * 256 + 256)
                vr, vi, ar, ai = products[4 * ((n - 1) % 2) : 4 * ((n - 1) % 2) + 4]
                total = sums.get((p, half), [jnp.zeros((8, 256), F32)] * 3)
                for c in range(r, r + ROWS, CHUNK):
                    some = slice(c, c + CHUNK)
                    mask = usable[some, cols]
                    ur, ui = mask * ar[some, :], mask * ai[some, :]
                    xr, xi = vr[some, :], vi[some, :]
                    terms = (xr * ur - xi * ui, xr * ui + xi * ur, ur * ur + ui * ui)
                    total = [s + jnp.sum(t.reshape(CHUNK // 8, 8, 256), axis=0) for s, t in zip(total, terms)]
                sums[p, half] = total
    for (p, half), total in sums.items():
        for n in range(3):
            acc[n, p, :, half * 256 : half * 256 + 256] = total[n]

    steps = []
    for part_id in range(2):
        for p in range(2):
            weight_sum = jnp.sum(acc[2, p], axis=0, keepdims=True)
            moment = jnp.sum(acc[part_id, p], axis=0, keepdims=True) * (1.0 / NFRAMES)
            own = near_gain[part_id * 2 + p : part_id * 2 + p + 1]
            steps.append((moment - own * weight_sum) / (1.0 + weight_sum))

    mine = (iota((16, 512), 1) & 15) == iota((16, 512), 0)
    placed = jnp.zeros((48, 128), F32)
    for n, value in enumerate(steps):
        value = jnp.where(mine, jnp.broadcast_to(value, (16, 512)), 0.0)
        hi = value.astype(BF)
        rest = value - hi.astype(F32)
        mid = rest.astype(BF)
        low = (rest - mid.astype(F32)).astype(BF)
        placed = placed + dot(jnp.concatenate([hi, mid, low], axis=0), move_ref[n])
    out_ref[...] = placed[0:16] + (placed[16:32] + placed[32:48])


def whole():
    return pl.BlockSpec(memory_space=pltpu.VMEM)


def held(x):
    return pltpu.with_memory_space_constraint(x, pltpu.HBM)


def anywhere():
    return pl.BlockSpec(memory_space=pltpu.HBM)


def make_spectra(channel, volts, gains, flags, positions, directions, weights):
    window, first, turn, second = filter_tables()
    operands = [volts, jnp.asarray(window), jnp.asarray(first), jnp.asarray(turn), jnp.asarray(second), gains, flags]
    operands = [held(x) for x in operands + [positions.T, directions.T, weights.T]]
    return pl.pallas_call(
        spectra_kernel,
        out_shape=(
            pltpu.VMEM((4 * CW, 128), BF),
            pltpu.VMEM((2, 2, 128, STATIONS), BF),
            pltpu.VMEM((STATIONS, 128), F32),
            pltpu.VMEM((STATIONS, 128), F32),
            pltpu.VMEM((STATIONS, 128), F32),
            pltpu.VMEM((STATIONS, 128), BF),
            pltpu.VMEM((128, 256), BF),
            pltpu.VMEM((16, 128), BF),
            pltpu.VMEM((4, STATIONS, 128), BF),
        ),
        in_specs=[pl.BlockSpec(memory_space=pltpu.SMEM)] + [anywhere()] * 10,
        out_specs=(whole(),) * 9,
        scratch_shapes=[
            pltpu.VMEM((CHUNKS, FRAMES_IN, 16, 128), BF),
            pltpu.VMEM((CHUNKS, TAPS, 16, 128), F32),
            pltpu.VMEM((384, 256), BF),
            pltpu.VMEM((2, 128, 128), F32),
            pltpu.VMEM((32, 256), BF),
            pltpu.VMEM((BLOCKS, 128), BF),
            pltpu.VMEM((SPB, STATIONS), jnp.int32),
            pltpu.VMEM((2, STATIONS), F32),
            pltpu.VMEM((2, SOURCES), F32),
            pltpu.VMEM((2, SOURCES), F32),
            pltpu.VMEM((8, 128), F32),
            pltpu.VMEM((STATIONS, 384), BF),
            pltpu.VMEM((NFRAMES, 128, 128), F32),
            pltpu.VMEM((NFRAMES * 128, 256), BF),
            pltpu.VMEM((NFRAMES * 128, 256), F32),
            pltpu.VMEM((256, NFRAMES * 128), BF),
            pltpu.VMEM((256, NFRAMES * 128), BF),
            pltpu.VMEM((256, 128), F32),
            pltpu.VMEM((4 * CW, 128), F32),
            pltpu.SemaphoreType.DMA((2, CHUNKS)),
            pltpu.SemaphoreType.DMA((8,)),
        ],
        compiler_params=pltpu.CompilerParams(vmem_limit_bytes=28 * 2**20),
        name="spectra",
    )(channel, *operands)


def arrange(voltages):
    rows = voltages.reshape(2, FRAMES_IN * 64, 128).transpose(1, 0, 2)
    return rows.reshape(FRAMES_IN, 128, 128)


def make_steps(index, recv, *prepared):
    return pl.pallas_call(
        pair_kernel,
        out_shape=jax.ShapeDtypeStruct((BLOCKS, 128), F32),
        in_specs=[pl.BlockSpec(memory_space=pltpu.SMEM)] + [whole()] * 9,
        out_specs=whole(),
        scratch_shapes=[
            pltpu.VMEM((4 * STATIONS, 128), F32),
            pltpu.VMEM((2, 2, 32, STATIONS), BF),
            pltpu.VMEM((2, STATIONS, 32), BF),
            pltpu.VMEM((2, STATIONS, 128), BF),
            pltpu.VMEM((STATIONS, STATIONS), F32),
            pltpu.VMEM((STATIONS, STATIONS), F32),
            pltpu.VMEM((3, 2, 8, STATIONS), F32),
        ]
        + [pltpu.VMEM((STATIONS, 256), F32)] * 8,
        compiler_params=pltpu.CompilerParams(vmem_limit_bytes=24 * 2**20),
        name="pairs",
    )(index, recv, *prepared)


def exchange(values, axes):
    return lax.all_to_all(values, axes, split_axis=0, concat_axis=0, tiled=True)


def body(voltages, station_gains, positions, directions, weights, baseline_flags):
    channel = jnp.reshape(lax.axis_index(CHAN) * BLOCKS + lax.axis_index(STN), (1,)).astype(jnp.int32)
    payload, *prepared = make_spectra(
        channel, arrange(voltages), station_gains[:, 0, :], baseline_flags, positions, directions, weights
    )
    recv = exchange(payload.reshape(CW, 4, 128), ORDER)
    steps = make_steps(channel, recv.reshape(4 * CW, 128), *prepared)
    return exchange(steps.reshape(BLOCKS, 1, 128), STN)


def solution(mesh):
    parts = Mesh(mesh.devices.reshape(8, 2, 2, 4, 4), CHAN + STN)
    in_specs = (P(STN, CHAN, None, None), P(CHAN, STN, None), P(), P(), P(), P(STN, None))
    out_specs = P(CHAN, STN, None)
    return jax.shard_map(body, mesh=parts, in_specs=in_specs, out_specs=out_specs, check_vma=False)
```

```python
import math

import jax
import jax.numpy as jnp
import numpy as np
from jax import lax
from jax.experimental import pallas as pl
from jax.experimental.pallas import tpu as pltpu
from jax.sharding import Mesh
from jax.sharding import PartitionSpec as P

F = 4096
CW = 512
FRAME = 8192
TAPS = 16
STATIONS = 512
NFRAMES = 16
SOURCES = 32
BLOCKS = 16
SPB = 32
FRAMES_IN = NFRAMES + TAPS - 1
CHUNKS = 8
CHUNK = 16
ROWS = 256
CHAN = ("y", "z_hi", "core")
STN = ("x", "z_lo")
ORDER = ("core", "y", "z_hi") + STN
BF = jnp.bfloat16
F32 = jnp.float32


def split_np(values):
    hi = values.astype(jnp.bfloat16)
    lo = (values - hi.astype(np.float64)).astype(jnp.bfloat16)
    return hi, lo


def filter_tables():
    n = np.arange(TAPS * FRAME, dtype=np.float64)
    q = (n + 0.5 - TAPS * FRAME / 2) / FRAME
    window = np.sin(np.pi * q) / (np.pi * q) * (0.5 - 0.5 * np.cos(2 * np.pi * n / (TAPS * FRAME)))
    window = window.astype(np.float32).reshape(TAPS, 64, 128)
    window = np.repeat(window, 2, axis=1).reshape(TAPS, CHUNKS, 16, 128).transpose(1, 0, 2, 3)
    j = np.arange(64)[:, None]
    k = np.arange(64)[None, :]
    angle = 2 * np.pi * (k * j % 64) / 64
    first = np.stack([np.cos(angle), -np.sin(angle)])
    first = np.einsum("cjk,st->jsctk", first, np.eye(2)).reshape(128, 256)
    hi, lo = split_np(first)
    first = np.concatenate([hi, hi, lo], axis=0)
    m = np.arange(128)[:, None]
    angle = 2 * np.pi * (k * m % 8192) / 8192
    turn = np.stack([np.cos(angle), np.sin(angle)])
    turn = np.concatenate([turn, turn], axis=2).astype(np.float32)
    b = np.arange(8)[:, None]
    m = np.arange(128)[None, :]
    angle = 2 * np.pi * (b * m % 128) / 128
    c = np.cos(angle) / math.sqrt(FRAME)
    s = np.sin(angle) / math.sqrt(FRAME)
    to_re = np.concatenate([c, s], axis=1)
    to_im = np.concatenate([-s, c], axis=1)
    second = np.stack([to_re, to_im], axis=1).reshape(16, 256)
    second = np.concatenate(split_np(second), axis=0)
    return window, first, turn, second


def split2(x):
    hi = x.astype(BF)
    return hi, (x - hi.astype(F32)).astype(BF)


def dot(a, b):
    return lax.dot_general(a, b, (((1,), (0,)), ((), ())), preferred_element_type=F32)


def dot_nt(a, b):
    return lax.dot_general(a, b, (((1,), (1,)), ((), ())), preferred_element_type=F32)


def iota(shape, dim):
    return lax.broadcasted_iota(jnp.int32, shape, dim)


def place_of(n):
    return (lax.shift_right_logical(n, 5) & 7) * 4 + (lax.shift_right_logical(n, 4) & 1) * 2 + lax.shift_right_logical(n, 8)


def number_of(channel):
    group = channel // BLOCKS
    return (group % 2) * 256 + (group // 4) * 32 + ((group // 2) % 2) * 16 + channel % BLOCKS


def sine_cosine(x):
    turns = jnp.floor(x * (2.0 / math.pi) + 0.5)
    r = x - turns * 1.5703125
    r = r - turns * 4.837512969970703125e-4
    r = r - turns * 7.54978995489188216e-8
    z = r * r
    sine = ((-1.9515295891e-4 * z + 8.3321608736e-3) * z - 1.6666654611e-1) * z * r + r
    cosine = ((2.443315711809948e-5 * z - 1.388731625493765e-3) * z + 4.166664568298827e-2) * z * z - 0.5 * z + 1.0
    quarter = turns.astype(jnp.int32) & 3
    odd = (quarter & 1) == 1
    sin = jnp.where(odd, cosine, sine)
    cos = jnp.where(odd, sine, cosine)
    sin = jnp.where(quarter >= 2, -sin, sin)
    cos = jnp.where((quarter == 1) | (quarter == 2), -cos, cos)
    return sin, cos


def prepare_steering(channel, position, columns, near_e, steer_ref, turned_ref):
    east, north = position[0:1, :], position[1:2, :]
    delays = columns[0:SOURCES, 0:1] * east + columns[0:SOURCES, 1:2] * north
    scaled = 2.0 * math.pi * (1.0 + channel.astype(F32) / F)
    sin, cos = sine_cosine(scaled * delays)
    parts = []
    for p in range(2):
        weight = columns[0:SOURCES, 2 + p : 3 + p]
        parts += [(cos * weight).astype(BF), (-sin * weight).astype(BF)]
    source, target = iota((STATIONS, STATIONS), 0), iota((1, STATIONS), 1)
    wanted = (target & 15) * SPB + place_of(target)
    ordered = dot(jnp.concatenate(parts, axis=0), jnp.where(source == wanted, 1.0, 0.0).astype(BF))
    steer, turned = [], []
    for p in range(2):
        re, im = ordered[p * 64 : p * 64 + 32], ordered[p * 64 + 32 : p * 64 + 64]
        steer += [re, im]
        turned += [-im, re]
        near_e[p, 0] = jnp.concatenate([re, im, re, im], axis=0).astype(BF)
        near_e[p, 1] = jnp.concatenate([-im, re, -im, re], axis=0).astype(BF)
    steer_ref[...] = jnp.concatenate(steer, axis=0).T
    turned_ref[...] = jnp.concatenate(turned, axis=0).T


def prepare_matrices(own_ref, row_ref, wide_ref, code_ref, move_ref):
    station = iota((STATIONS, 128), 0)
    lane = iota((STATIONS, 128), 1)
    place, block = place_of(station), station & 15
    own_ref[...] = jnp.where(lax.shift_right_logical(lane & 63, 1) == place, 1.0, 0.0)
    row_ref[...] = jnp.where(block == lane, 1.0, 0.0).astype(BF)
    source = iota((128, 256), 0)
    target = iota((128, 256), 1)
    fits = ((source & 1) == (lax.shift_right_logical(target, 6) & 1)) & (
        lax.shift_right_logical(source, 6) == lax.shift_right_logical(target, 7)
    )
    wide_ref[...] = jnp.where(fits, 1.0, 0.0).astype(BF)
    code = iota((16, 128), 0)
    lane = iota((16, 128), 1)
    fits = ((lane & 1) == (code & 1)) & (lax.shift_right_logical(lane, 6) == lax.shift_right_logical(code, 1))
    code_ref[...] = jnp.where(fits, 1.0, 0.0).astype(BF)
    for n in range(4):
        column = (n // 2) * 64 + place * 2 + (n % 2)
        move_ref[n] = jnp.where(iota((STATIONS, 128), 1) == column, 1.0, 0.0).astype(BF)


def spectra_kernel(
    index_ref,
    volt_ref,
    win_ref,
    first_ref,
    turn_ref,
    second_ref,
    gain_ref,
    flag_ref,
    position_ref,
    direction_ref,
    weight_ref,
    out_ref,
    near_e,
    steer_ref,
    turned_ref,
    own_ref,
    row_ref,
    wide_ref,
    code_ref,
    move_ref,
    volts,
    window,
    first,
    turn,
    second,
    gain,
    flag,
    position,
    direction,
    weight,
    table,
    pick,
    fold,
    left,
    section,
    high,
    low,
    gathered,
    part,
    sems,
    late,
):
    def volt_copy(step):
        rows = pl.ds(pl.multiple_of(step * 16, 16), 16)
        return pltpu.make_async_copy(volt_ref.at[:, rows, :], volts.at[step], sems.at[0, step])

    def window_copy(step):
        return pltpu.make_async_copy(win_ref.at[step], window.at[step], sems.at[1, step])

    others = [
        pltpu.make_async_copy(source, target, late.at[n])
        for n, (source, target) in enumerate(
            ((first_ref, first), (turn_ref, turn), (second_ref, second), (gain_ref, gain), (flag_ref, flag))
        )
    ]
    small = [
        pltpu.make_async_copy(position_ref, position, late.at[5]),
        pltpu.make_async_copy(direction_ref, direction, late.at[6]),
        pltpu.make_async_copy(weight_ref, weight, late.at[7]),
    ]
    table[...] = jnp.zeros((8, 128), F32)
    for copy in small:
        copy.start()
    for step in range(CHUNKS):
        volt_copy(step).start()
        window_copy(step).start()
    for copy in others:
        copy.start()

    channel = index_ref[0]
    index = channel // BLOCKS
    place = (iota((1, 384), 1) + 64 * (number_of(channel) // 64)) & (STATIONS - 1)
    wanted = (place & 15) * SPB + place_of(place)
    pick[...] = jnp.where(iota((STATIONS, 384), 0) == wanted, 1.0, 0.0).astype(BF)

    prepare_matrices(own_ref, row_ref, wide_ref, code_ref, move_ref)

    def chunk(step, carry):
        volt_copy(step).wait()
        window_copy(step).wait()
        x = volts[step].astype(F32)
        acc = x[0:NFRAMES] * window[step, 0][None]
        for tap in range(1, TAPS):
            acc = acc + x[tap : tap + NFRAMES] * window[step, tap][None]
        fold[:, pl.ds(pl.multiple_of(step * 16, 16), 16), :] = acc
        return carry

    lax.fori_loop(0, CHUNKS, chunk, 0)
    for copy in small:
        copy.wait()
    table[0:2, 0:SOURCES] = direction[...]
    table[2:4, 0:SOURCES] = weight[...]
    prepare_steering(channel, position[...], table[...].T, near_e, steer_ref, turned_ref)
    for copy in others:
        copy.wait()

    turn_cos = turn[0]
    turn_sin = turn[1]
    for t in range(NFRAMES):
        hi, lo = split2(fold[t].T)
        rows = slice(t * 128, t * 128 + 128)
        left[rows, 0:128] = hi
        left[rows, 128:256] = lo
    for group in range(4):
        rows = slice(group * 512, group * 512 + 512)
        section[rows, :] = dot(left[rows, :], first[0:256]) + dot(left[rows, 0:128], first[256:384])
    for t in range(NFRAMES):
        rows = slice(t * 128, t * 128 + 128)
        re = section[rows, 0:128]
        im = section[rows, 128:256]
        for part_id, value in enumerate((re * turn_cos + im * turn_sin, im * turn_cos - re * turn_sin)):
            hi, lo = split2(value)
            place = slice(part_id * 128, part_id * 128 + 128)
            high[place, rows] = hi
            low[place, rows] = lo
    main = dot(second[...], high[...])
    rest = dot(second[0:16], low[...])
    value = main[0:16] + (main[16:32] + rest)
    for t in range(NFRAMES):
        gathered[pl.ds(t, 16, stride=16), :] = value[:, t * 128 : t * 128 + 128]
    total = gathered[0:256].T

    flags = jnp.broadcast_to(flag[pl.ds(index, 1), :].astype(F32), (8, STATIONS)).astype(BF)
    row = dot(flags, pick[...])[0:1]

    for b in range(8):
        lanes = [
            total[0:64, b * 32 : b * 32 + 32],
            total[64:128, b * 32 : b * 32 + 32],
            jnp.broadcast_to(row[:, 0:64], (64, 64)),
        ]
        rows = jnp.concatenate(lanes, axis=1)
        for n in range(4):
            target = (n % 2) * 256 + b * 32 + (n // 2) * 16
            part[pl.ds(target * 4, 16, stride=4), :] = rows[n * 16 : n * 16 + 16]
    part[pl.ds(1, 512, stride=4), :] = jnp.broadcast_to(row[:, 64:192], (512, 128))
    part[pl.ds(2, 512, stride=4), :] = jnp.broadcast_to(row[:, 192:320], (512, 128))
    gains = gain[...].astype(F32)
    for i in range(32):
        part[pl.ds(i * 64 + 3, 16, stride=4), :] = gains
    out_ref[...] = part[0 : 4 * CW, :].astype(BF)


def pair_kernel(
    index_ref,
    recv_ref,
    near_e,
    steer_ref,
    turned_ref,
    own_ref,
    row_ref,
    wide_ref,
    code_ref,
    move_ref,
    out_ref,
    part,
    near_x,
    far_x,
    far_e,
    brought,
    usable,
    acc,
    *products,
):
    part[0 : 4 * STATIONS, :] = recv_ref[...].astype(F32)
    first = part[pl.ds(0, 512, stride=4), :]
    channel = index_ref[0]

    sent = jnp.concatenate(
        [
            first[:, 64:128],
            part[pl.ds(1, 512, stride=4), :],
            part[pl.ds(2, 512, stride=4), :],
        ],
        axis=1,
    )
    empty = jnp.zeros((64, 64), F32)
    for a in range(8):
        pieces = []
        for b in range(8):
            d = (b - a) % 8
            pieces.append(sent[a * 64 : a * 64 + 64, d * 64 : d * 64 + 64] if d <= 4 else empty)
        brought[pl.ds(a * 64, 64), :] = jnp.concatenate(pieces, axis=1)
    turned = brought[...].T
    low = iota((64, 128), 1) < 64
    for a in range(8):
        rows = slice(a * 64, a * 64 + 64)
        for b in range(0, 8, 2):
            cols = slice(b * 64, b * 64 + 128)
            direct, back = brought[rows, cols], turned[rows, cols]
            known = [(n - a) % 8 <= 4 for n in (b, b + 1)]
            if known == [True, True]:
                both = direct
            elif known == [False, False]:
                both = back
            else:
                both = jnp.where(low == known[0], direct, back)
            if a // 2 == b // 2:
                both = jnp.where(iota((64, 128), 0) + (a - b) * 64 == iota((64, 128), 1), 0.0, both)
            usable[rows, cols] = both

    xt = first.T
    for p in range(2):
        own = xt[p * 32 : p * 32 + 32]
        near_x[p, 0] = own.astype(BF)
        near_x[p, 1] = jnp.concatenate([own[16:32], -own[0:16]], axis=0).astype(BF)
        far_x[p] = first[:, p * 32 : p * 32 + 32].astype(BF)

    gains = part[pl.ds((number_of(channel) - channel % BLOCKS) * 4 + 3, 16, stride=4), :].astype(BF)
    gains = jnp.concatenate([gains, jnp.zeros((112, 128), BF)], axis=0)
    spread = (dot(row_ref[...], gains) * own_ref[...]).astype(BF)
    wide = dot(spread, wide_ref[...])
    scaled = wide[:, 0:128] * steer_ref[...] + wide[:, 128:256] * turned_ref[...]
    for q in range(2):
        hi, lo = split2(scaled[:, q * 64 : q * 64 + 64])
        far_e[q] = jnp.concatenate([hi, lo], axis=1)
    near_gain = dot_nt(code_ref[...], spread)

    blocks = [(p, half, q) for p in range(2) for half in range(2) for q in range(2)]
    sums = {}
    for n in range(len(blocks) + 1):
        for r in range(0, STATIONS, ROWS):
            rows = slice(r, r + ROWS)
            if n < len(blocks):
                p, half, q = blocks[n]
                cols = slice(half * 256, half * 256 + 256)
                vr, vi, ar, ai = products[4 * (n % 2) : 4 * (n % 2) + 4]
                vr[rows, :] = dot(far_x[q, rows], near_x[p, 0, :, cols])
                vi[rows, :] = dot(far_x[q, rows], near_x[p, 1, :, cols])
                ar[rows, :] = dot(far_e[q, rows], near_e[p, 0, :, cols])
                ai[rows, :] = dot(far_e[q, rows], near_e[p, 1, :, cols])
            if n > 0:
                p, half, q = blocks[n - 1]
                cols = slice(half * 256, half * 256 + 256)
                vr, vi, ar, ai = products[4 * ((n - 1) % 2) : 4 * ((n - 1) % 2) + 4]
                total = sums.get((p, half), [jnp.zeros((8, 256), F32)] * 3)
                for c in range(r, r + ROWS, CHUNK):
                    some = slice(c, c + CHUNK)
                    mask = usable[some, cols]
                    ur, ui = mask * ar[some, :], mask * ai[some, :]
                    xr, xi = vr[some, :], vi[some, :]
                    terms = (xr * ur - xi * ui, xr * ui + xi * ur, ur * ur + ui * ui)
                    total = [s + jnp.sum(t.reshape(CHUNK // 8, 8, 256), axis=0) for s, t in zip(total, terms)]
                sums[p, half] = total
    for (p, half), total in sums.items():
        for n in range(3):
            acc[n, p, :, half * 256 : half * 256 + 256] = total[n]

    steps = []
    for part_id in range(2):
        for p in range(2):
            weight_sum = jnp.sum(acc[2, p], axis=0, keepdims=True)
            moment = jnp.sum(acc[part_id, p], axis=0, keepdims=True) * (1.0 / NFRAMES)
            own = near_gain[part_id * 2 + p : part_id * 2 + p + 1]
            steps.append((moment - own * weight_sum) / (1.0 + weight_sum))

    mine = (iota((16, 512), 1) & 15) == iota((16, 512), 0)
    placed = jnp.zeros((48, 128), F32)
    for n, value in enumerate(steps):
        value = jnp.where(mine, jnp.broadcast_to(value, (16, 512)), 0.0)
        hi = value.astype(BF)
        rest = value - hi.astype(F32)
        mid = rest.astype(BF)
        low = (rest - mid.astype(F32)).astype(BF)
        placed = placed + dot(jnp.concatenate([hi, mid, low], axis=0), move_ref[n])
    out_ref[...] = placed[0:16] + (placed[16:32] + placed[32:48])


def whole():
    return pl.BlockSpec(memory_space=pltpu.VMEM)


def held(x):
    return pltpu.with_memory_space_constraint(x, pltpu.HBM)


def anywhere():
    return pl.BlockSpec(memory_space=pltpu.HBM)


def make_spectra(channel, volts, gains, flags, positions, directions, weights):
    window, first, turn, second = filter_tables()
    operands = [volts, jnp.asarray(window), jnp.asarray(first), jnp.asarray(turn), jnp.asarray(second), gains, flags]
    operands = [held(x) for x in operands + [positions.T, directions.T, weights.T]]
    return pl.pallas_call(
        spectra_kernel,
        out_shape=(
            pltpu.VMEM((4 * CW, 128), BF),
            pltpu.VMEM((2, 2, 128, STATIONS), BF),
            pltpu.VMEM((STATIONS, 128), F32),
            pltpu.VMEM((STATIONS, 128), F32),
            pltpu.VMEM((STATIONS, 128), F32),
            pltpu.VMEM((STATIONS, 128), BF),
            pltpu.VMEM((128, 256), BF),
            pltpu.VMEM((16, 128), BF),
            pltpu.VMEM((4, STATIONS, 128), BF),
        ),
        in_specs=[pl.BlockSpec(memory_space=pltpu.SMEM)] + [anywhere()] * 10,
        out_specs=(whole(),) * 9,
        scratch_shapes=[
            pltpu.VMEM((CHUNKS, FRAMES_IN, 16, 128), BF),
            pltpu.VMEM((CHUNKS, TAPS, 16, 128), F32),
            pltpu.VMEM((384, 256), BF),
            pltpu.VMEM((2, 128, 128), F32),
            pltpu.VMEM((32, 256), BF),
            pltpu.VMEM((BLOCKS, 128), BF),
            pltpu.VMEM((SPB, STATIONS), jnp.int32),
            pltpu.VMEM((2, STATIONS), F32),
            pltpu.VMEM((2, SOURCES), F32),
            pltpu.VMEM((2, SOURCES), F32),
            pltpu.VMEM((8, 128), F32),
            pltpu.VMEM((STATIONS, 384), BF),
            pltpu.VMEM((NFRAMES, 128, 128), F32),
            pltpu.VMEM((NFRAMES * 128, 256), BF),
            pltpu.VMEM((NFRAMES * 128, 256), F32),
            pltpu.VMEM((256, NFRAMES * 128), BF),
            pltpu.VMEM((256, NFRAMES * 128), BF),
            pltpu.VMEM((256 + 16, 128), F32),
            pltpu.VMEM((4 * CW + 64, 128), F32),
            pltpu.SemaphoreType.DMA((2, CHUNKS)),
            pltpu.SemaphoreType.DMA((8,)),
        ],
        compiler_params=pltpu.CompilerParams(vmem_limit_bytes=28 * 2**20),
        name="spectra",
    )(channel, *operands)


def arrange(voltages):
    rows = voltages.reshape(2, FRAMES_IN * 64, 128).transpose(1, 0, 2)
    return rows.reshape(FRAMES_IN, 128, 128)


def make_steps(index, recv, *prepared):
    return pl.pallas_call(
        pair_kernel,
        out_shape=jax.ShapeDtypeStruct((BLOCKS, 128), F32),
        in_specs=[pl.BlockSpec(memory_space=pltpu.SMEM)] + [whole()] * 9,
        out_specs=whole(),
        scratch_shapes=[
            pltpu.VMEM((4 * STATIONS + 64, 128), F32),
            pltpu.VMEM((2, 2, 32, STATIONS), BF),
            pltpu.VMEM((2, STATIONS, 32), BF),
            pltpu.VMEM((2, STATIONS, 128), BF),
            pltpu.VMEM((STATIONS, STATIONS), F32),
            pltpu.VMEM((STATIONS, STATIONS), F32),
            pltpu.VMEM((3, 2, 8, STATIONS), F32),
        ]
        + [pltpu.VMEM((STATIONS, 256), F32)] * 8,
        compiler_params=pltpu.CompilerParams(vmem_limit_bytes=24 * 2**20),
        name="pairs",
    )(index, recv, *prepared)


def exchange(values, axes):
    return lax.all_to_all(values, axes, split_axis=0, concat_axis=0, tiled=True)


def body(voltages, station_gains, positions, directions, weights, baseline_flags):
    channel = jnp.reshape(lax.axis_index(CHAN) * BLOCKS + lax.axis_index(STN), (1,)).astype(jnp.int32)
    payload, *prepared = make_spectra(
        channel, arrange(voltages), station_gains[:, 0, :], baseline_flags, positions, directions, weights
    )
    recv = exchange(payload.reshape(CW, 4, 128), ORDER)
    steps = make_steps(channel, recv.reshape(4 * CW, 128), *prepared)
    return exchange(steps.reshape(BLOCKS, 1, 128), STN)


def solution(mesh):
    parts = Mesh(mesh.devices.reshape(8, 2, 2, 4, 4), CHAN + STN)
    in_specs = (P(STN, CHAN, None, None), P(CHAN, STN, None), P(), P(), P(), P(STN, None))
    out_specs = P(CHAN, STN, None)
    return jax.shard_map(body, mesh=parts, in_specs=in_specs, out_specs=out_specs, check_vma=False)
```

```python
import math

import jax
import jax.numpy as jnp
import numpy as np
from jax import lax
from jax.experimental import pallas as pl
from jax.experimental.pallas import tpu as pltpu
from jax.sharding import Mesh
from jax.sharding import PartitionSpec as P

F = 4096
CW = 512
FRAME = 8192
TAPS = 16
STATIONS = 512
NFRAMES = 16
SOURCES = 32
BLOCKS = 16
SPB = 32
FRAMES_IN = NFRAMES + TAPS - 1
CHUNKS = 8
CHUNK = 16
ROWS = 256
CHAN = ("y", "z_hi", "core")
STN = ("x", "z_lo")
ORDER = ("y", "z_hi") + STN + ("core",)
BF = jnp.bfloat16
F32 = jnp.float32


def split_np(values):
    hi = values.astype(jnp.bfloat16)
    lo = (values - hi.astype(np.float64)).astype(jnp.bfloat16)
    return hi, lo


def filter_tables():
    n = np.arange(TAPS * FRAME, dtype=np.float64)
    q = (n + 0.5 - TAPS * FRAME / 2) / FRAME
    window = np.sin(np.pi * q) / (np.pi * q) * (0.5 - 0.5 * np.cos(2 * np.pi * n / (TAPS * FRAME)))
    window = window.astype(np.float32).reshape(TAPS, 64, 128)
    window = np.repeat(window, 2, axis=1).reshape(TAPS, CHUNKS, 16, 128).transpose(1, 0, 2, 3)
    j = np.arange(64)[:, None]
    k = np.arange(64)[None, :]
    angle = 2 * np.pi * (k * j % 64) / 64
    first = np.stack([np.cos(angle), -np.sin(angle)])
    first = np.einsum("cjk,st->jsctk", first, np.eye(2)).reshape(128, 256)
    hi, lo = split_np(first)
    first = np.concatenate([hi, hi, lo], axis=0)
    m = np.arange(128)[:, None]
    angle = 2 * np.pi * (k * m % 8192) / 8192
    turn = np.stack([np.cos(angle), np.sin(angle)])
    turn = np.concatenate([turn, turn], axis=2).astype(np.float32)
    b = np.arange(8)[:, None]
    m = np.arange(128)[None, :]
    angle = 2 * np.pi * (b * m % 128) / 128
    c = np.cos(angle) / math.sqrt(FRAME)
    s = np.sin(angle) / math.sqrt(FRAME)
    to_re = np.concatenate([c, s], axis=1)
    to_im = np.concatenate([-s, c], axis=1)
    second = np.stack([to_re, to_im], axis=1).reshape(16, 256)
    second = np.concatenate(split_np(second), axis=0)
    return window, first, turn, second


def split2(x):
    hi = x.astype(BF)
    return hi, (x - hi.astype(F32)).astype(BF)


def dot(a, b):
    return lax.dot_general(a, b, (((1,), (0,)), ((), ())), preferred_element_type=F32)


def dot_nt(a, b):
    return lax.dot_general(a, b, (((1,), (1,)), ((), ())), preferred_element_type=F32)


def iota(shape, dim):
    return lax.broadcasted_iota(jnp.int32, shape, dim)


def place_of(n):
    return lax.shift_right_logical(n, 6) * 4 + (lax.shift_right_logical(n, 5) & 1) * 2 + (n & 1)


def block_of(n):
    return lax.shift_right_logical(n, 1) & (BLOCKS - 1)


def number_of(channel):
    group = channel // BLOCKS
    return (group // 2) * 32 + (channel % BLOCKS) * 2 + group % 2


def sine_cosine(x):
    turns = jnp.floor(x * (2.0 / math.pi) + 0.5)
    r = x - turns * 1.5703125
    r = r - turns * 4.837512969970703125e-4
    r = r - turns * 7.54978995489188216e-8
    z = r * r
    sine = ((-1.9515295891e-4 * z + 8.3321608736e-3) * z - 1.6666654611e-1) * z * r + r
    cosine = ((2.443315711809948e-5 * z - 1.388731625493765e-3) * z + 4.166664568298827e-2) * z * z - 0.5 * z + 1.0
    quarter = turns.astype(jnp.int32) & 3
    odd = (quarter & 1) == 1
    sin = jnp.where(odd, cosine, sine)
    cos = jnp.where(odd, sine, cosine)
    sin = jnp.where(quarter >= 2, -sin, sin)
    cos = jnp.where((quarter == 1) | (quarter == 2), -cos, cos)
    return sin, cos


def prepare_steering(channel, position, columns, near_e, steer_ref, turned_ref):
    east, north = position[0:1, :], position[1:2, :]
    delays = columns[0:SOURCES, 0:1] * east + columns[0:SOURCES, 1:2] * north
    scaled = 2.0 * math.pi * (1.0 + channel.astype(F32) / F)
    sin, cos = sine_cosine(scaled * delays)
    parts = []
    for p in range(2):
        weight = columns[0:SOURCES, 2 + p : 3 + p]
        parts += [(cos * weight).astype(BF), (-sin * weight).astype(BF)]
    source, target = iota((STATIONS, STATIONS), 0), iota((1, STATIONS), 1)
    wanted = block_of(target) * SPB + place_of(target)
    ordered = dot(jnp.concatenate(parts, axis=0), jnp.where(source == wanted, 1.0, 0.0).astype(BF))
    steer, turned = [], []
    for p in range(2):
        re, im = ordered[p * 64 : p * 64 + 32], ordered[p * 64 + 32 : p * 64 + 64]
        steer += [re, im]
        turned += [-im, re]
        near_e[p, 0] = jnp.concatenate([re, im, re, im], axis=0).astype(BF)
        near_e[p, 1] = jnp.concatenate([-im, re, -im, re], axis=0).astype(BF)
    steer_ref[...] = jnp.concatenate(steer, axis=0).T
    turned_ref[...] = jnp.concatenate(turned, axis=0).T


def prepare_matrices(own_ref, row_ref, wide_ref, code_ref, move_ref):
    station = iota((STATIONS, 128), 0)
    lane = iota((STATIONS, 128), 1)
    place, block = place_of(station), block_of(station)
    own_ref[...] = jnp.where(lax.shift_right_logical(lane & 63, 1) == place, 1.0, 0.0)
    row_ref[...] = jnp.where(block == lane, 1.0, 0.0).astype(BF)
    source = iota((128, 256), 0)
    target = iota((128, 256), 1)
    fits = ((source & 1) == (lax.shift_right_logical(target, 6) & 1)) & (
        lax.shift_right_logical(source, 6) == lax.shift_right_logical(target, 7)
    )
    wide_ref[...] = jnp.where(fits, 1.0, 0.0).astype(BF)
    code = iota((16, 128), 0)
    lane = iota((16, 128), 1)
    fits = ((lane & 1) == (code & 1)) & (lax.shift_right_logical(lane, 6) == lax.shift_right_logical(code, 1))
    code_ref[...] = jnp.where(fits, 1.0, 0.0).astype(BF)
    for n in range(4):
        column = (n // 2) * 64 + place * 2 + (n % 2)
        move_ref[n] = jnp.where(iota((STATIONS, 128), 1) == column, 1.0, 0.0).astype(BF)


def spectra_kernel(
    index_ref,
    volt_ref,
    win_ref,
    first_ref,
    turn_ref,
    second_ref,
    gain_ref,
    flag_ref,
    position_ref,
    direction_ref,
    weight_ref,
    out_ref,
    near_e,
    steer_ref,
    turned_ref,
    own_ref,
    row_ref,
    wide_ref,
    code_ref,
    move_ref,
    volts,
    window,
    first,
    turn,
    second,
    gain,
    flag,
    position,
    direction,
    weight,
    table,
    pick,
    fold,
    left,
    section,
    high,
    low,
    gathered,
    part,
    sems,
    late,
):
    def volt_copy(step):
        rows = pl.ds(pl.multiple_of(step * 16, 16), 16)
        return pltpu.make_async_copy(volt_ref.at[:, rows, :], volts.at[step], sems.at[0, step])

    def window_copy(step):
        return pltpu.make_async_copy(win_ref.at[step], window.at[step], sems.at[1, step])

    others = [
        pltpu.make_async_copy(source, target, late.at[n])
        for n, (source, target) in enumerate(
            ((first_ref, first), (turn_ref, turn), (second_ref, second), (gain_ref, gain), (flag_ref, flag))
        )
    ]
    small = [
        pltpu.make_async_copy(position_ref, position, late.at[5]),
        pltpu.make_async_copy(direction_ref, direction, late.at[6]),
        pltpu.make_async_copy(weight_ref, weight, late.at[7]),
    ]
    table[...] = jnp.zeros((8, 128), F32)
    for copy in small:
        copy.start()
    for step in range(CHUNKS):
        volt_copy(step).start()
        window_copy(step).start()
    for copy in others:
        copy.start()

    channel = index_ref[0]
    index = channel // BLOCKS
    place = (iota((1, 384), 1) + 64 * (number_of(channel) // 64)) & (STATIONS - 1)
    wanted = block_of(place) * SPB + place_of(place)
    pick[...] = jnp.where(iota((STATIONS, 384), 0) == wanted, 1.0, 0.0).astype(BF)

    prepare_matrices(own_ref, row_ref, wide_ref, code_ref, move_ref)

    def chunk(step, carry):
        volt_copy(step).wait()
        window_copy(step).wait()
        x = volts[step].astype(F32)
        acc = x[0:NFRAMES] * window[step, 0][None]
        for tap in range(1, TAPS):
            acc = acc + x[tap : tap + NFRAMES] * window[step, tap][None]
        fold[:, pl.ds(pl.multiple_of(step * 16, 16), 16), :] = acc
        return carry

    lax.fori_loop(0, CHUNKS, chunk, 0)
    for copy in small:
        copy.wait()
    table[0:2, 0:SOURCES] = direction[...]
    table[2:4, 0:SOURCES] = weight[...]
    prepare_steering(channel, position[...], table[...].T, near_e, steer_ref, turned_ref)
    for copy in others:
        copy.wait()

    turn_cos = turn[0]
    turn_sin = turn[1]
    for t in range(NFRAMES):
        hi, lo = split2(fold[t].T)
        rows = slice(t * 128, t * 128 + 128)
        left[rows, 0:128] = hi
        left[rows, 128:256] = lo
    for group in range(4):
        rows = slice(group * 512, group * 512 + 512)
        section[rows, :] = dot(left[rows, :], first[0:256]) + dot(left[rows, 0:128], first[256:384])
    for t in range(NFRAMES):
        rows = slice(t * 128, t * 128 + 128)
        re = section[rows, 0:128]
        im = section[rows, 128:256]
        for part_id, value in enumerate((re * turn_cos + im * turn_sin, im * turn_cos - re * turn_sin)):
            hi, lo = split2(value)
            place = slice(part_id * 128, part_id * 128 + 128)
            high[place, rows] = hi
            low[place, rows] = lo
    main = dot(second[...], high[...])
    rest = dot(second[0:16], low[...])
    value = main[0:16] + (main[16:32] + rest)
    for t in range(NFRAMES):
        gathered[pl.ds(t, 16, stride=16), :] = value[:, t * 128 : t * 128 + 128]
    total = gathered[0:256].T

    flags = jnp.broadcast_to(flag[pl.ds(index, 1), :].astype(F32), (8, STATIONS)).astype(BF)
    row = dot(flags, pick[...])[0:1]

    for b in range(8):
        lanes = [
            total[0:64, b * 32 : b * 32 + 32],
            total[64:128, b * 32 : b * 32 + 32],
            jnp.broadcast_to(row[:, 0:64], (64, 64)),
        ]
        rows = jnp.concatenate(lanes, axis=1)
        for n in range(4):
            target = b * 64 + (n // 2) * 32 + n % 2
            part[pl.ds(target * 4, 16, stride=8), :] = rows[n * 16 : n * 16 + 16]
    part[pl.ds(1, 512, stride=4), :] = jnp.broadcast_to(row[:, 64:192], (512, 128))
    part[pl.ds(2, 512, stride=4), :] = jnp.broadcast_to(row[:, 192:320], (512, 128))
    gains = gain[...].astype(F32)
    for i in range(32):
        part[pl.ds((i // 2) * 128 + (i % 2) * 4 + 3, 16, stride=8), :] = gains
    out_ref[...] = part[0 : 4 * CW, :].astype(BF)


def pair_kernel(
    index_ref,
    recv_ref,
    near_e,
    steer_ref,
    turned_ref,
    own_ref,
    row_ref,
    wide_ref,
    code_ref,
    move_ref,
    out_ref,
    part,
    near_x,
    far_x,
    far_e,
    brought,
    usable,
    acc,
    *products,
):
    part[0 : 4 * STATIONS, :] = recv_ref[...].astype(F32)
    first = part[pl.ds(0, 512, stride=4), :]
    channel = index_ref[0]

    sent = jnp.concatenate(
        [
            first[:, 64:128],
            part[pl.ds(1, 512, stride=4), :],
            part[pl.ds(2, 512, stride=4), :],
        ],
        axis=1,
    )
    empty = jnp.zeros((64, 64), F32)
    for a in range(8):
        pieces = []
        for b in range(8):
            d = (b - a) % 8
            pieces.append(sent[a * 64 : a * 64 + 64, d * 64 : d * 64 + 64] if d <= 4 else empty)
        brought[pl.ds(a * 64, 64), :] = jnp.concatenate(pieces, axis=1)
    turned = brought[...].T
    low = iota((64, 128), 1) < 64
    for a in range(8):
        rows = slice(a * 64, a * 64 + 64)
        for b in range(0, 8, 2):
            cols = slice(b * 64, b * 64 + 128)
            direct, back = brought[rows, cols], turned[rows, cols]
            known = [(n - a) % 8 <= 4 for n in (b, b + 1)]
            if known == [True, True]:
                both = direct
            elif known == [False, False]:
                both = back
            else:
                both = jnp.where(low == known[0], direct, back)
            if a // 2 == b // 2:
                both = jnp.where(iota((64, 128), 0) + (a - b) * 64 == iota((64, 128), 1), 0.0, both)
            usable[rows, cols] = both

    xt = first.T
    for p in range(2):
        own = xt[p * 32 : p * 32 + 32]
        near_x[p, 0] = own.astype(BF)
        near_x[p, 1] = jnp.concatenate([own[16:32], -own[0:16]], axis=0).astype(BF)
        far_x[p] = first[:, p * 32 : p * 32 + 32].astype(BF)

    gains = part[pl.ds(number_of(channel - channel % BLOCKS) * 4 + 3, 16, stride=8), :].astype(BF)
    gains = jnp.concatenate([gains, jnp.zeros((112, 128), BF)], axis=0)
    spread = (dot(row_ref[...], gains) * own_ref[...]).astype(BF)
    wide = dot(spread, wide_ref[...])
    scaled = wide[:, 0:128] * steer_ref[...] + wide[:, 128:256] * turned_ref[...]
    for q in range(2):
        hi, lo = split2(scaled[:, q * 64 : q * 64 + 64])
        far_e[q] = jnp.concatenate([hi, lo], axis=1)
    near_gain = dot_nt(code_ref[...], spread)

    blocks = [(p, half, q) for p in range(2) for half in range(2) for q in range(2)]
    sums = {}
    for n in range(len(blocks) + 1):
        for r in range(0, STATIONS, ROWS):
            rows = slice(r, r + ROWS)
            if n < len(blocks):
                p, half, q = blocks[n]
                cols = slice(half * 256, half * 256 + 256)
                vr, vi, ar, ai = products[4 * (n % 2) : 4 * (n % 2) + 4]
                vr[rows, :] = dot(far_x[q, rows], near_x[p, 0, :, cols])
                vi[rows, :] = dot(far_x[q, rows], near_x[p, 1, :, cols])
                ar[rows, :] = dot(far_e[q, rows], near_e[p, 0, :, cols])
                ai[rows, :] = dot(far_e[q, rows], near_e[p, 1, :, cols])
            if n > 0:
                p, half, q = blocks[n - 1]
                cols = slice(half * 256, half * 256 + 256)
                vr, vi, ar, ai = products[4 * ((n - 1) % 2) : 4 * ((n - 1) % 2) + 4]
                total = sums.get((p, half), [jnp.zeros((8, 256), F32)] * 3)
                for c in range(r, r + ROWS, CHUNK):
                    some = slice(c, c + CHUNK)
                    mask = usable[some, cols]
                    ur, ui = mask * ar[some, :], mask * ai[some, :]
                    xr, xi = vr[some, :], vi[some, :]
                    terms = (xr * ur - xi * ui, xr * ui + xi * ur, ur * ur + ui * ui)
                    total = [s + jnp.sum(t.reshape(CHUNK // 8, 8, 256), axis=0) for s, t in zip(total, terms)]
                sums[p, half] = total
    for (p, half), total in sums.items():
        for n in range(3):
            acc[n, p, :, half * 256 : half * 256 + 256] = total[n]

    steps = []
    for part_id in range(2):
        for p in range(2):
            weight_sum = jnp.sum(acc[2, p], axis=0, keepdims=True)
            moment = jnp.sum(acc[part_id, p], axis=0, keepdims=True) * (1.0 / NFRAMES)
            own = near_gain[part_id * 2 + p : part_id * 2 + p + 1]
            steps.append((moment - own * weight_sum) / (1.0 + weight_sum))

    mine = block_of(iota((16, 512), 1)) == iota((16, 512), 0)
    placed = jnp.zeros((48, 128), F32)
    for n, value in enumerate(steps):
        value = jnp.where(mine, jnp.broadcast_to(value, (16, 512)), 0.0)
        hi = value.astype(BF)
        rest = value - hi.astype(F32)
        mid = rest.astype(BF)
        low = (rest - mid.astype(F32)).astype(BF)
        placed = placed + dot(jnp.concatenate([hi, mid, low], axis=0), move_ref[n])
    out_ref[...] = placed[0:16] + (placed[16:32] + placed[32:48])


def whole():
    return pl.BlockSpec(memory_space=pltpu.VMEM)


def held(x):
    return pltpu.with_memory_space_constraint(x, pltpu.HBM)


def anywhere():
    return pl.BlockSpec(memory_space=pltpu.HBM)


def make_spectra(channel, volts, gains, flags, positions, directions, weights):
    window, first, turn, second = filter_tables()
    operands = [volts, jnp.asarray(window), jnp.asarray(first), jnp.asarray(turn), jnp.asarray(second), gains, flags]
    operands = [held(x) for x in operands + [positions.T, directions.T, weights.T]]
    return pl.pallas_call(
        spectra_kernel,
        out_shape=(
            pltpu.VMEM((4 * CW, 128), BF),
            pltpu.VMEM((2, 2, 128, STATIONS), BF),
            pltpu.VMEM((STATIONS, 128), F32),
            pltpu.VMEM((STATIONS, 128), F32),
            pltpu.VMEM((STATIONS, 128), F32),
            pltpu.VMEM((STATIONS, 128), BF),
            pltpu.VMEM((128, 256), BF),
            pltpu.VMEM((16, 128), BF),
            pltpu.VMEM((4, STATIONS, 128), BF),
        ),
        in_specs=[pl.BlockSpec(memory_space=pltpu.SMEM)] + [anywhere()] * 10,
        out_specs=(whole(),) * 9,
        scratch_shapes=[
            pltpu.VMEM((CHUNKS, FRAMES_IN, 16, 128), BF),
            pltpu.VMEM((CHUNKS, TAPS, 16, 128), F32),
            pltpu.VMEM((384, 256), BF),
            pltpu.VMEM((2, 128, 128), F32),
            pltpu.VMEM((32, 256), BF),
            pltpu.VMEM((BLOCKS, 128), BF),
            pltpu.VMEM((SPB, STATIONS), jnp.int32),
            pltpu.VMEM((2, STATIONS), F32),
            pltpu.VMEM((2, SOURCES), F32),
            pltpu.VMEM((2, SOURCES), F32),
            pltpu.VMEM((8, 128), F32),
            pltpu.VMEM((STATIONS, 384), BF),
            pltpu.VMEM((NFRAMES, 128, 128), F32),
            pltpu.VMEM((NFRAMES * 128, 256), BF),
            pltpu.VMEM((NFRAMES * 128, 256), F32),
            pltpu.VMEM((256, NFRAMES * 128), BF),
            pltpu.VMEM((256, NFRAMES * 128), BF),
            pltpu.VMEM((256 + 16, 128), F32),
            pltpu.VMEM((4 * CW + 64, 128), F32),
            pltpu.SemaphoreType.DMA((2, CHUNKS)),
            pltpu.SemaphoreType.DMA((8,)),
        ],
        compiler_params=pltpu.CompilerParams(vmem_limit_bytes=28 * 2**20),
        name="spectra",
    )(channel, *operands)


def arrange(voltages):
    rows = voltages.reshape(2, FRAMES_IN * 64, 128).transpose(1, 0, 2)
    return rows.reshape(FRAMES_IN, 128, 128)


def make_steps(index, recv, *prepared):
    return pl.pallas_call(
        pair_kernel,
        out_shape=jax.ShapeDtypeStruct((BLOCKS, 128), F32),
        in_specs=[pl.BlockSpec(memory_space=pltpu.SMEM)] + [whole()] * 9,
        out_specs=whole(),
        scratch_shapes=[
            pltpu.VMEM((4 * STATIONS + 64, 128), F32),
            pltpu.VMEM((2, 2, 32, STATIONS), BF),
            pltpu.VMEM((2, STATIONS, 32), BF),
            pltpu.VMEM((2, STATIONS, 128), BF),
            pltpu.VMEM((STATIONS, STATIONS), F32),
            pltpu.VMEM((STATIONS, STATIONS), F32),
            pltpu.VMEM((3, 2, 8, STATIONS), F32),
        ]
        + [pltpu.VMEM((STATIONS, 256), F32)] * 8,
        compiler_params=pltpu.CompilerParams(vmem_limit_bytes=24 * 2**20),
        name="pairs",
    )(index, recv, *prepared)


def exchange(values, axes):
    return lax.all_to_all(values, axes, split_axis=0, concat_axis=0, tiled=True)


def body(voltages, station_gains, positions, directions, weights, baseline_flags):
    channel = jnp.reshape(lax.axis_index(CHAN) * BLOCKS + lax.axis_index(STN), (1,)).astype(jnp.int32)
    payload, *prepared = make_spectra(
        channel, arrange(voltages), station_gains[:, 0, :], baseline_flags, positions, directions, weights
    )
    recv = exchange(payload.reshape(CW, 4, 128), ORDER)
    steps = make_steps(channel, recv.reshape(4 * CW, 128), *prepared)
    return exchange(steps.reshape(BLOCKS, 1, 128), STN)


def solution(mesh):
    parts = Mesh(mesh.devices.reshape(8, 2, 2, 4, 4), CHAN + STN)
    in_specs = (P(STN, CHAN, None, None), P(CHAN, STN, None), P(), P(), P(), P(STN, None))
    out_specs = P(CHAN, STN, None)
    return jax.shard_map(body, mesh=parts, in_specs=in_specs, out_specs=out_specs, check_vma=False)
```

```python
import math

import jax
import jax.numpy as jnp
import numpy as np
from jax import lax
from jax.experimental import pallas as pl
from jax.experimental.pallas import tpu as pltpu
from jax.sharding import PartitionSpec as P

F = 4096
CW = 512
FRAME = 8192
TAPS = 16
STATIONS = 512
NFRAMES = 16
SOURCES = 32
BLOCKS = 16
SPB = 32
FRAMES_IN = NFRAMES + TAPS - 1
CHUNKS = 8
CHUNK = 16
ROWS = 256
BF = jnp.bfloat16
F32 = jnp.float32


def split_np(values):
    hi = values.astype(jnp.bfloat16)
    lo = (values - hi.astype(np.float64)).astype(jnp.bfloat16)
    return hi, lo


def filter_tables():
    n = np.arange(TAPS * FRAME, dtype=np.float64)
    q = (n + 0.5 - TAPS * FRAME / 2) / FRAME
    window = np.sin(np.pi * q) / (np.pi * q) * (0.5 - 0.5 * np.cos(2 * np.pi * n / (TAPS * FRAME)))
    window = window.astype(np.float32).reshape(TAPS, 64, 128)
    window = np.repeat(window, 2, axis=1).reshape(TAPS, CHUNKS, 16, 128).transpose(1, 0, 2, 3)
    j = np.arange(64)[:, None]
    k = np.arange(64)[None, :]
    angle = 2 * np.pi * (k * j % 64) / 64
    first = np.stack([np.cos(angle), -np.sin(angle)])
    first = np.einsum("cjk,st->jsctk", first, np.eye(2)).reshape(128, 256)
    hi, lo = split_np(first)
    first = np.concatenate([hi, hi, lo], axis=0)
    m = np.arange(128)[:, None]
    angle = 2 * np.pi * (k * m % 8192) / 8192
    turn = np.stack([np.cos(angle), np.sin(angle)])
    turn = np.concatenate([turn, turn], axis=2).astype(np.float32)
    b = np.arange(8)[:, None]
    m = np.arange(128)[None, :]
    angle = 2 * np.pi * (b * m % 128) / 128
    c = np.cos(angle) / math.sqrt(FRAME)
    s = np.sin(angle) / math.sqrt(FRAME)
    to_re = np.concatenate([c, s], axis=1)
    to_im = np.concatenate([-s, c], axis=1)
    second = np.stack([to_re, to_im], axis=1).reshape(16, 256)
    second = np.concatenate(split_np(second), axis=0)
    return window, first, turn, second


def split2(x):
    hi = x.astype(BF)
    return hi, (x - hi.astype(F32)).astype(BF)


def dot(a, b):
    return lax.dot_general(a, b, (((1,), (0,)), ((), ())), preferred_element_type=F32)


def dot_nt(a, b):
    return lax.dot_general(a, b, (((1,), (1,)), ((), ())), preferred_element_type=F32)


def iota(shape, dim):
    return lax.broadcasted_iota(jnp.int32, shape, dim)


def sine_cosine(x):
    turns = jnp.floor(x * (2.0 / math.pi) + 0.5)
    r = x - turns * 1.5703125
    r = r - turns * 4.837512969970703125e-4
    r = r - turns * 7.54978995489188216e-8
    z = r * r
    sine = ((-1.9515295891e-4 * z + 8.3321608736e-3) * z - 1.6666654611e-1) * z * r + r
    cosine = ((2.443315711809948e-5 * z - 1.388731625493765e-3) * z + 4.166664568298827e-2) * z * z - 0.5 * z + 1.0
    quarter = turns.astype(jnp.int32) & 3
    odd = (quarter & 1) == 1
    sin = jnp.where(odd, cosine, sine)
    cos = jnp.where(odd, sine, cosine)
    sin = jnp.where(quarter >= 2, -sin, sin)
    cos = jnp.where((quarter == 1) | (quarter == 2), -cos, cos)
    return sin, cos


def prepare_steering(channel, position, columns, near_e, steer_ref, turned_ref):
    east, north = position[0:1, :], position[1:2, :]
    delays = columns[0:SOURCES, 0:1] * east + columns[0:SOURCES, 1:2] * north
    scaled = 2.0 * math.pi * (1.0 + channel.astype(F32) / F)
    sin, cos = sine_cosine(scaled * delays)
    parts = []
    for p in range(2):
        weight = columns[0:SOURCES, 2 + p : 3 + p]
        parts += [(cos * weight).astype(BF), (-sin * weight).astype(BF)]
    steer, turned = [], []
    for p in range(2):
        re, im = parts[2 * p].astype(F32), parts[2 * p + 1].astype(F32)
        steer += [re, im]
        turned += [-im, re]
        near_e[p, 0] = jnp.concatenate([re, im, re, im], axis=0).astype(BF)
        near_e[p, 1] = jnp.concatenate([-im, re, -im, re], axis=0).astype(BF)
    steer_ref[...] = jnp.concatenate(steer, axis=0).T
    turned_ref[...] = jnp.concatenate(turned, axis=0).T


def prepare_matrices(own_ref, row_ref, wide_ref, code_ref, move_ref):
    station = iota((STATIONS, 128), 0)
    lane = iota((STATIONS, 128), 1)
    place, block = station & (SPB - 1), lax.shift_right_logical(station, 5)
    own_ref[...] = jnp.where(lax.shift_right_logical(lane & 63, 1) == place, 1.0, 0.0)
    row_ref[...] = jnp.where(block == lane, 1.0, 0.0).astype(BF)
    source = iota((128, 256), 0)
    target = iota((128, 256), 1)
    fits = ((source & 1) == (lax.shift_right_logical(target, 6) & 1)) & (
        lax.shift_right_logical(source, 6) == lax.shift_right_logical(target, 7)
    )
    wide_ref[...] = jnp.where(fits, 1.0, 0.0).astype(BF)
    code = iota((16, 128), 0)
    lane = iota((16, 128), 1)
    fits = ((lane & 1) == (code & 1)) & (lax.shift_right_logical(lane, 6) == lax.shift_right_logical(code, 1))
    code_ref[...] = jnp.where(fits, 1.0, 0.0).astype(BF)
    for n in range(4):
        column = (n // 2) * 64 + place * 2 + (n % 2)
        move_ref[n] = jnp.where(iota((STATIONS, 128), 1) == column, 1.0, 0.0).astype(BF)


def spectra_kernel(
    index_ref,
    volt_ref,
    win_ref,
    first_ref,
    turn_ref,
    second_ref,
    gain_ref,
    flag_ref,
    position_ref,
    direction_ref,
    weight_ref,
    out_ref,
    near_e,
    steer_ref,
    turned_ref,
    own_ref,
    row_ref,
    wide_ref,
    code_ref,
    move_ref,
    volts,
    window,
    first,
    turn,
    second,
    gain,
    flag,
    position,
    direction,
    weight,
    table,
    pick,
    fold,
    left,
    section,
    high,
    low,
    gathered,
    part,
    sems,
    late,
):
    def volt_copy(step):
        rows = pl.ds(pl.multiple_of(step * 16, 16), 16)
        return pltpu.make_async_copy(volt_ref.at[:, rows, :], volts.at[step], sems.at[0, step])

    def window_copy(step):
        return pltpu.make_async_copy(win_ref.at[step], window.at[step], sems.at[1, step])

    others = [
        pltpu.make_async_copy(source, target, late.at[n])
        for n, (source, target) in enumerate(
            ((first_ref, first), (turn_ref, turn), (second_ref, second), (gain_ref, gain), (flag_ref, flag))
        )
    ]
    small = [
        pltpu.make_async_copy(position_ref, position, late.at[5]),
        pltpu.make_async_copy(direction_ref, direction, late.at[6]),
        pltpu.make_async_copy(weight_ref, weight, late.at[7]),
    ]
    table[...] = jnp.zeros((8, 128), F32)
    for copy in small:
        copy.start()
    for step in range(CHUNKS):
        volt_copy(step).start()
        window_copy(step).start()
    for copy in others:
        copy.start()

    channel = index_ref[0]
    index = channel // BLOCKS
    place = (iota((1, 384), 1) + 64 * ((channel % BLOCKS) // 2)) & (STATIONS - 1)
    pick[...] = jnp.where(iota((STATIONS, 384), 0) == place, 1.0, 0.0).astype(BF)

    prepare_matrices(own_ref, row_ref, wide_ref, code_ref, move_ref)

    def chunk(step, carry):
        volt_copy(step).wait()
        window_copy(step).wait()
        x = volts[step].astype(F32)
        acc = x[0:NFRAMES] * window[step, 0][None]
        for tap in range(1, TAPS):
            acc = acc + x[tap : tap + NFRAMES] * window[step, tap][None]
        fold[:, pl.ds(pl.multiple_of(step * 16, 16), 16), :] = acc
        return carry

    lax.fori_loop(0, CHUNKS, chunk, 0)
    for copy in small:
        copy.wait()
    table[0:2, 0:SOURCES] = direction[...]
    table[2:4, 0:SOURCES] = weight[...]
    prepare_steering(channel, position[...], table[...].T, near_e, steer_ref, turned_ref)
    for copy in others:
        copy.wait()

    turn_cos = turn[0]
    turn_sin = turn[1]
    for t in range(NFRAMES):
        hi, lo = split2(fold[t].T)
        rows = slice(t * 128, t * 128 + 128)
        left[rows, 0:128] = hi
        left[rows, 128:256] = lo
    for group in range(4):
        rows = slice(group * 512, group * 512 + 512)
        section[rows, :] = dot(left[rows, :], first[0:256]) + dot(left[rows, 0:128], first[256:384])
    for t in range(NFRAMES):
        rows = slice(t * 128, t * 128 + 128)
        re = section[rows, 0:128]
        im = section[rows, 128:256]
        for part_id, value in enumerate((re * turn_cos + im * turn_sin, im * turn_cos - re * turn_sin)):
            hi, lo = split2(value)
            place = slice(part_id * 128, part_id * 128 + 128)
            high[place, rows] = hi
            low[place, rows] = lo
    main = dot(second[...], high[...])
    rest = dot(second[0:16], low[...])
    value = main[0:16] + (main[16:32] + rest)
    for t in range(NFRAMES):
        gathered[pl.ds(t, 16, stride=16), :] = value[:, t * 128 : t * 128 + 128]
    total = gathered[...].T

    flags = jnp.broadcast_to(flag[pl.ds(index, 1), :].astype(F32), (8, STATIONS)).astype(BF)
    row = dot(flags, pick[...])[0:1]

    for b in range(8):
        lanes = [
            total[0:64, b * 32 : b * 32 + 32],
            total[64:128, b * 32 : b * 32 + 32],
            jnp.broadcast_to(row[:, 0:64], (64, 64)),
        ]
        rows = jnp.concatenate(lanes, axis=1)
        for n in range(4):
            part[pl.ds((4 * b + n) * 4, 16, stride=128), :] = rows[n * 16 : n * 16 + 16]
    part[pl.ds(1, 512, stride=4), :] = jnp.broadcast_to(row[:, 64:192], (512, 128))
    part[pl.ds(2, 512, stride=4), :] = jnp.broadcast_to(row[:, 192:320], (512, 128))
    gains = gain[...].astype(F32)
    for i in range(32):
        part[pl.ds(i * 4 + 3, 16, stride=128), :] = gains
    out_ref[...] = part[...].astype(BF)


def pair_kernel(
    index_ref,
    recv_ref,
    near_e,
    steer_ref,
    turned_ref,
    own_ref,
    row_ref,
    wide_ref,
    code_ref,
    move_ref,
    out_ref,
    part,
    near_x,
    far_x,
    far_e,
    brought,
    usable,
    acc,
    *products,
):
    part[...] = recv_ref[...].astype(F32)
    first = part[pl.ds(0, 512, stride=4), :]
    index = index_ref[0] // BLOCKS

    sent = jnp.concatenate(
        [
            first[:, 64:128],
            part[pl.ds(1, 512, stride=4), :],
            part[pl.ds(2, 512, stride=4), :],
        ],
        axis=1,
    )
    empty = jnp.zeros((64, 64), F32)
    for a in range(8):
        pieces = []
        for b in range(8):
            d = (b - a) % 8
            pieces.append(sent[a * 64 : a * 64 + 64, d * 64 : d * 64 + 64] if d <= 4 else empty)
        brought[pl.ds(a * 64, 64), :] = jnp.concatenate(pieces, axis=1)
    turned = brought[...].T
    low = iota((64, 128), 1) < 64
    for a in range(8):
        rows = slice(a * 64, a * 64 + 64)
        for b in range(0, 8, 2):
            cols = slice(b * 64, b * 64 + 128)
            direct, back = brought[rows, cols], turned[rows, cols]
            known = [(n - a) % 8 <= 4 for n in (b, b + 1)]
            if known == [True, True]:
                both = direct
            elif known == [False, False]:
                both = back
            else:
                both = jnp.where(low == known[0], direct, back)
            if a // 2 == b // 2:
                both = jnp.where(iota((64, 128), 0) + (a - b) * 64 == iota((64, 128), 1), 0.0, both)
            usable[rows, cols] = both

    xt = first.T
    for p in range(2):
        own = xt[p * 32 : p * 32 + 32]
        near_x[p, 0] = own.astype(BF)
        near_x[p, 1] = jnp.concatenate([own[16:32], -own[0:16]], axis=0).astype(BF)
        far_x[p] = first[:, p * 32 : p * 32 + 32].astype(BF)

    gains = part[pl.ds(index * 4 + 3, 16, stride=128), :].astype(BF)
    gains = jnp.concatenate([gains, jnp.zeros((112, 128), BF)], axis=0)
    spread = (dot(row_ref[...], gains) * own_ref[...]).astype(BF)
    wide = dot(spread, wide_ref[...])
    scaled = wide[:, 0:128] * steer_ref[...] + wide[:, 128:256] * turned_ref[...]
    for q in range(2):
        hi, lo = split2(scaled[:, q * 64 : q * 64 + 64])
        far_e[q] = jnp.concatenate([hi, lo], axis=1)
    near_gain = dot_nt(code_ref[...], spread)

    blocks = [(p, half, q) for p in range(2) for half in range(2) for q in range(2)]
    sums = {}
    for n in range(len(blocks) + 1):
        for r in range(0, STATIONS, ROWS):
            rows = slice(r, r + ROWS)
            if n < len(blocks):
                p, half, q = blocks[n]
                cols = slice(half * 256, half * 256 + 256)
                vr, vi, ar, ai = products[4 * (n % 2) : 4 * (n % 2) + 4]
                vr[rows, :] = dot(far_x[q, rows], near_x[p, 0, :, cols])
                vi[rows, :] = dot(far_x[q, rows], near_x[p, 1, :, cols])
                ar[rows, :] = dot(far_e[q, rows], near_e[p, 0, :, cols])
                ai[rows, :] = dot(far_e[q, rows], near_e[p, 1, :, cols])
            if n > 0:
                p, half, q = blocks[n - 1]
                cols = slice(half * 256, half * 256 + 256)
                vr, vi, ar, ai = products[4 * ((n - 1) % 2) : 4 * ((n - 1) % 2) + 4]
                total = sums.get((p, half), [jnp.zeros((8, 256), F32)] * 3)
                for c in range(r, r + ROWS, CHUNK):
                    some = slice(c, c + CHUNK)
                    mask = usable[some, cols]
                    ur, ui = mask * ar[some, :], mask * ai[some, :]
                    xr, xi = vr[some, :], vi[some, :]
                    terms = (xr * ur - xi * ui, xr * ui + xi * ur, ur * ur + ui * ui)
                    total = [s + jnp.sum(t.reshape(CHUNK // 8, 8, 256), axis=0) for s, t in zip(total, terms)]
                sums[p, half] = total
    for (p, half), total in sums.items():
        for n in range(3):
            acc[n, p, :, half * 256 : half * 256 + 256] = total[n]

    steps = []
    for part_id in range(2):
        for p in range(2):
            weight_sum = jnp.sum(acc[2, p], axis=0, keepdims=True)
            moment = jnp.sum(acc[part_id, p], axis=0, keepdims=True) * (1.0 / NFRAMES)
            own = near_gain[part_id * 2 + p : part_id * 2 + p + 1]
            steps.append((moment - own * weight_sum) / (1.0 + weight_sum))

    mine = lax.shift_right_logical(iota((16, 512), 1), 5) == iota((16, 512), 0)
    placed = jnp.zeros((48, 128), F32)
    for n, value in enumerate(steps):
        value = jnp.where(mine, jnp.broadcast_to(value, (16, 512)), 0.0)
        hi = value.astype(BF)
        rest = value - hi.astype(F32)
        mid = rest.astype(BF)
        low = (rest - mid.astype(F32)).astype(BF)
        placed = placed + dot(jnp.concatenate([hi, mid, low], axis=0), move_ref[n])
    out_ref[...] = placed[0:16] + (placed[16:32] + placed[32:48])


def whole():
    return pl.BlockSpec(memory_space=pltpu.VMEM)


def held(x):
    return pltpu.with_memory_space_constraint(x, pltpu.HBM)


def anywhere():
    return pl.BlockSpec(memory_space=pltpu.HBM)


def make_spectra(channel, volts, gains, flags, positions, directions, weights):
    window, first, turn, second = filter_tables()
    operands = [volts, jnp.asarray(window), jnp.asarray(first), jnp.asarray(turn), jnp.asarray(second), gains, flags]
    operands = [held(x) for x in operands + [positions.T, directions.T, weights.T]]
    return pl.pallas_call(
        spectra_kernel,
        out_shape=(
            pltpu.VMEM((4 * CW, 128), BF),
            pltpu.VMEM((2, 2, 128, STATIONS), BF),
            pltpu.VMEM((STATIONS, 128), F32),
            pltpu.VMEM((STATIONS, 128), F32),
            pltpu.VMEM((STATIONS, 128), F32),
            pltpu.VMEM((STATIONS, 128), BF),
            pltpu.VMEM((128, 256), BF),
            pltpu.VMEM((16, 128), BF),
            pltpu.VMEM((4, STATIONS, 128), BF),
        ),
        in_specs=[pl.BlockSpec(memory_space=pltpu.SMEM)] + [anywhere()] * 10,
        out_specs=(whole(),) * 9,
        scratch_shapes=[
            pltpu.VMEM((CHUNKS, FRAMES_IN, 16, 128), BF),
            pltpu.VMEM((CHUNKS, TAPS, 16, 128), F32),
            pltpu.VMEM((384, 256), BF),
            pltpu.VMEM((2, 128, 128), F32),
            pltpu.VMEM((32, 256), BF),
            pltpu.VMEM((BLOCKS, 128), BF),
            pltpu.VMEM((SPB, STATIONS), jnp.int32),
            pltpu.VMEM((2, STATIONS), F32),
            pltpu.VMEM((2, SOURCES), F32),
            pltpu.VMEM((2, SOURCES), F32),
            pltpu.VMEM((8, 128), F32),
            pltpu.VMEM((STATIONS, 384), BF),
            pltpu.VMEM((NFRAMES, 128, 128), F32),
            pltpu.VMEM((NFRAMES * 128, 256), BF),
            pltpu.VMEM((NFRAMES * 128, 256), F32),
            pltpu.VMEM((256, NFRAMES * 128), BF),
            pltpu.VMEM((256, NFRAMES * 128), BF),
            pltpu.VMEM((256, 128), F32),
            pltpu.VMEM((4 * CW, 128), F32),
            pltpu.SemaphoreType.DMA((2, CHUNKS)),
            pltpu.SemaphoreType.DMA((8,)),
        ],
        compiler_params=pltpu.CompilerParams(vmem_limit_bytes=28 * 2**20),
        name="spectra",
    )(channel, *operands)


def arrange(voltages):
    rows = voltages.reshape(2, FRAMES_IN * 64, 128).transpose(1, 0, 2)
    return rows.reshape(FRAMES_IN, 128, 128)


def make_steps(index, recv, *prepared):
    return pl.pallas_call(
        pair_kernel,
        out_shape=jax.ShapeDtypeStruct((BLOCKS, 128), F32),
        in_specs=[pl.BlockSpec(memory_space=pltpu.SMEM)] + [whole()] * 9,
        out_specs=whole(),
        scratch_shapes=[
            pltpu.VMEM((4 * STATIONS, 128), F32),
            pltpu.VMEM((2, 2, 32, STATIONS), BF),
            pltpu.VMEM((2, STATIONS, 32), BF),
            pltpu.VMEM((2, STATIONS, 128), BF),
            pltpu.VMEM((STATIONS, STATIONS), F32),
            pltpu.VMEM((STATIONS, STATIONS), F32),
            pltpu.VMEM((3, 2, 8, STATIONS), F32),
        ]
        + [pltpu.VMEM((STATIONS, 256), F32)] * 8,
        compiler_params=pltpu.CompilerParams(vmem_limit_bytes=24 * 2**20),
        name="pairs",
    )(index, recv, *prepared)


def body(voltages, station_gains, positions, directions, weights, baseline_flags):
    channel = jnp.reshape(lax.axis_index("chan") * BLOCKS + lax.axis_index("stn"), (1,)).astype(jnp.int32)
    payload, *prepared = make_spectra(
        channel, arrange(voltages), station_gains[:, 0, :], baseline_flags, positions, directions, weights
    )
    recv = lax.all_to_all(
        payload.reshape(CW, 4, 128), ("stn", "chan"), split_axis=0, concat_axis=0, tiled=True
    )
    steps = make_steps(channel, recv.reshape(4 * CW, 128), *prepared)
    return lax.all_to_all(steps.reshape(BLOCKS, 1, 128), "stn", split_axis=0, concat_axis=0, tiled=True)


def solution(mesh):
    in_specs = (P("stn", "chan", None, None), P("chan", "stn", None), P(), P(), P(), P("stn", None))
    out_specs = P("chan", "stn", None)
    return jax.shard_map(body, mesh=mesh, in_specs=in_specs, out_specs=out_specs, check_vma=False)
```
